32 devices in a mesh: row: 4 (over y, x), col: 8 (over z, core).
Axes of the slice: x: 2, y: 2, z: 4, core: 2. Of those that a mesh axis runs over, the one named last changes fastest.
Arguments:
- dofs: float32 [504, 8192], P(None, ('row', 'col')), may hold values from -6 to 6
- star: float32 [243, 8192], P(None, ('row', 'col')), may hold values from -1.25 to 1.25
- flux_mats: float32 [648, 8192], P(None, ('row', 'col')), may hold values from -0.75 to 0.75
- kxi: float32 [3, 56, 56], replicated, may hold values from -0.75 to 0.75
- face_proj: float32 [4, 56, 21], replicated, may hold values from -0.75 to 0.75
- face_lift: float32 [4, 21, 56], replicated, may hold values from -1.25 to 1.25
- orient: float32 [3, 21, 21], replicated, may hold values from -1.25 to 1.25
- neighbour: int32 [4, 8192], P(None, ('row', 'col')), may hold values from 0 to 2047
- orient_code: int32 [4, 8192], P(None, ('row', 'col')), may hold values from 0 to 2
- send_list: int32 [4, 2048], P(None, ('row', 'col')), may hold values from 0 to 255
- fault_part: int32 [4096, 1], P(('row', 'col')), may hold values from 0 to 31; in each aligned block of 128 rows (0 to 127, 128 to 255, ...) at most 8 rows name the same one
- fault_item: int32 [4096], P(('row', 'col')), may hold values from 0 to 1023
- shear_init: float32 [21, 4096], P(None, ('row', 'col')), may hold values from -8 to 8
- normal_init: float32 [21, 4096], P(None, ('row', 'col')), may hold values from 1 to 8
- state_var: float32 [21, 4096], P(None, ('row', 'col')), may hold values from 0.3 to 0.7
- slip_prev: float32 [21, 4096], P(None, ('row', 'col')), may hold values from 0.05 to 2
Outputs:
- dofs_next: float32 [504, 8192], P(None, ('row', 'col'))
- slip_rate: float32 [21, 4096], P(None, ('row', 'col'))
The draws below stay inside these ranges and needn't reach their ends.
Inputs may be any that keep to these rules, and one draw needn't show every extreme that they name: `fault_part`: partitions are numbered r * 8 + c. Among the 128 fault rows held by one device, no partition is named by more than 8 rows.
All inputs are finite; a program needn't handle non-finite values.
Results may differ from the reference program's by a relative error of at most 0.0003.
Values sent between devices are 32-bit elements; how exact they have to be, the bound alone decides.
No kernel may reach another device: no remote copies, remote signals or barrier semaphores. Data moves between devices by JAX's collectives and lax.ppermute only.
A program may use at most 128 MiB of HBM per device.

```python
import math
import jax
import jax.numpy as jnp
import numpy as np
from jax import lax

QUANT = 9
BASIS = 56
FACE_BASIS = 21
ORDER = 6
NEWTON_ITERS = 3
ELEM_DEV = 256
FAULT_DEV = 128
GHOSTS = 64
MOST = 8
ELEMENTS = 8192
SENDS = 2048
FAULTS = 4096
N_ROW = 4
N_COL = 8


def plant(values, own_key, low, high):
    longest = values.shape.index(max(values.shape))
    spots = []
    for shift in (0, 1):
        where = [jax.random.randint(jax.random.fold_in(own_key, axis), (), 0, length) for axis, length in enumerate(values.shape)]
        where[longest] = (where[longest] + shift) % values.shape[longest]
        spots.append(tuple(where))
    return values.at[spots[0]].set(low).at[spots[1]].set(high)


def shard_levels(own_key, shape, shards, smallest, high):
    def one(axis_at, parts):
        steps = jax.random.uniform(jax.random.fold_in(jax.random.fold_in(own_key, 6), axis_at), (parts,), jnp.float32, smallest / len(shards), high / len(shards))
        return jnp.repeat(jnp.exp(steps), shape[axis_at] // parts).reshape((-1,) + (1,) * (len(shape) - axis_at - 1))

    factor_of = one(*shards[0])
    for cut in shards[1:]:
        factor_of = factor_of * one(*cut)
    return factor_of


def routed_block(rng, own, number, rows, amount, top, reach, slope):
    order = jax.random.permutation(rng, amount)
    heavy_load, ordinary = shares(amount, rows * top, reach, slope, True), shares(amount, rows * top, reach, slope, False)
    places = jnp.arange(amount)

    def named(lengths, rotation):
        used = int((lengths > 0).sum())
        fixed = max(1, used // 4)
        moved = fixed + (places - fixed + rotation * (used - fixed)) % max(1, amount - fixed)
        return jnp.zeros((amount,), jnp.int32).at[order[jnp.where(places < fixed, places, moved)]].set(jnp.asarray(lengths, jnp.int32))

    lengths = jnp.where(number % 4 == 0, named(heavy_load, number // 4), named(ordinary, number - number // 4 - 1))
    mixed = jax.random.permutation(jax.random.fold_in(own, 3), amount)
    giver, sink = mixed[0:amount // 2 * 2:2], mixed[1:amount // 2 * 2:2]
    margin = jnp.minimum(lengths[giver] - 1, reach - lengths[sink]) // 2
    margin = jnp.where((giver == order[0]) | (sink == order[0]) | (lengths[sink] == 0), 0, jnp.maximum(margin, 0))
    moved = jax.random.randint(jax.random.fold_in(own, 4), (amount // 2,), 0, 1 << 20) % (margin + 1)
    lengths = lengths.at[giver].add(-moved).at[sink].add(moved)
    items = jnp.searchsorted(jnp.cumsum(lengths), jnp.arange(rows * top), side="right").astype(jnp.int32)
    grid = items.reshape(top, rows).T
    grid = grid[jax.random.permutation(jax.random.fold_in(own, 1), rows)]
    rotation = jax.random.randint(jax.random.fold_in(own, 2), (rows, 1), 0, top)
    return jnp.take_along_axis(grid, (jnp.arange(top)[None, :] + rotation) % top, axis=1)


def shares(count, total, limit, skew, full):
    portions = [(1 << 20) // math.isqrt(grade ** skew) + 1 for grade in range(1, count + 1)]
    largest = limit if full else min(limit, max(-(-total // count), total * portions[0] // sum(portions)))
    least = 1 if total - largest >= count - 1 else 0
    holding, surplus = [largest] + [least] * (count - 1), total - largest - least * (count - 1)
    while surplus > 0:
        movable = [i for i in range(1, count) if holding[i] < largest] or [i for i in range(1, count) if holding[i] < limit]
        whole, remaining = sum([portions[i] for i in movable]), surplus
        for i in movable:
            addition = min(limit - holding[i], max(1, remaining * portions[i] // whole), surplus)
            holding[i] = holding[i] + addition
            surplus = surplus - addition
    return np.array(holding)


def scatter_about(rng, extent, scale, bound, cuts=(), kind=jnp.bfloat16):
    result = jax.random.normal(rng, extent, jnp.float32) * scale
    if len(cuts) > 0:
        result = shard_levels(rng, extent, cuts, -0.22, 0.18) * result
    return jnp.clip(result, min=-bound, max=bound).astype(kind)


def setup_inputs(seed: int = 0) -> dict:
    key_list = jax.random.split(jax.random.key(seed), 17)
    dofs = scatter_about(key_list[0], (QUANT * BASIS, ELEMENTS), 1.0, 6.0, ((1, 32),), jnp.float32)
    star = scatter_about(key_list[1], (3 * QUANT * QUANT, ELEMENTS), (3 * QUANT) ** -0.5, 1.25, ((1, 32),), jnp.float32)
    flux_mats = scatter_about(key_list[2], (8 * QUANT * QUANT, ELEMENTS), (8 * QUANT) ** -0.5, 0.75, ((1, 32),), jnp.float32)
    kxi = scatter_about(key_list[3], (3, BASIS, BASIS), BASIS ** -0.5, 0.75, (), jnp.float32)
    face_proj = scatter_about(key_list[4], (4, BASIS, FACE_BASIS), BASIS ** -0.5, 0.75, (), jnp.float32)
    face_lift = scatter_about(key_list[5], (4, FACE_BASIS, BASIS), FACE_BASIS ** -0.5, 1.25, (), jnp.float32)
    orient = scatter_about(key_list[6], (3, FACE_BASIS, FACE_BASIS), FACE_BASIS ** -0.5, 1.25, (), jnp.float32)
    neighbour = plant(jax.random.randint(key_list[7], (4, ELEMENTS), 0, 4 * ELEM_DEV + 16 * GHOSTS), jax.random.fold_in(key_list[7], 1), 0, (4 * ELEM_DEV + 16 * GHOSTS) - 1).astype(jnp.int32)
    orient_code = plant(jax.random.randint(key_list[8], (4, ELEMENTS), 0, 3), jax.random.fold_in(key_list[8], 1), 0, 2).astype(jnp.int32)
    send_list = plant(jax.random.randint(key_list[9], (4, SENDS), 0, ELEM_DEV), jax.random.fold_in(key_list[9], 1), 0, ELEM_DEV - 1).astype(jnp.int32)
    fault_part_keys = jax.random.split(jax.random.fold_in(key_list[10], 1), FAULTS // FAULT_DEV)
    fault_part_turns = jax.random.permutation(jax.random.fold_in(key_list[10], 3), FAULTS // FAULT_DEV)
    fault_part = jax.vmap(lambda own, number: routed_block(jax.random.fold_in(key_list[10], 2), own, number, FAULT_DEV, N_ROW * N_COL, 1, MOST, 2))(fault_part_keys, fault_part_turns).reshape((FAULTS, 1))
    fault_item = plant(jax.random.randint(key_list[11], (FAULTS,), 0, 4 * ELEM_DEV), jax.random.fold_in(key_list[11], 1), 0, (4 * ELEM_DEV) - 1).astype(jnp.int32)
    shear_init = scatter_about(key_list[12], (FACE_BASIS, FAULTS), 2.0, 8.0, ((1, 32),), jnp.float32)
    normal_init = jnp.clip(jnp.exp(math.log(8.0) - 2.0794415 * jax.random.uniform(key_list[13], (FACE_BASIS, FAULTS), jnp.float32) ** shard_levels(key_list[13], (FACE_BASIS, FAULTS), ((1, 32),), -0.2, 0.2)), 1.0, 8.0)
    state_var = jnp.clip(0.3 + 0.39999998 * jax.random.uniform(key_list[14], (FACE_BASIS, FAULTS), jnp.float32) ** shard_levels(key_list[14], (FACE_BASIS, FAULTS), ((1, 32),), -0.2, 0.2), 0.3, 0.7)
    slip_prev = jnp.clip(0.05 + 1.95 * jax.random.uniform(key_list[15], (FACE_BASIS, FAULTS), jnp.float32) ** shard_levels(key_list[15], (FACE_BASIS, FAULTS), ((1, 32),), -0.2, 0.2), 0.05, 2.0)
    return dict(dofs=dofs, star=star, flux_mats=flux_mats, kxi=kxi, face_proj=face_proj, face_lift=face_lift, orient=orient, neighbour=neighbour, orient_code=orient_code, send_list=send_list, fault_part=fault_part, fault_item=fault_item, shear_init=shear_init, normal_init=normal_init, state_var=state_var, slip_prev=slip_prev)


time_step = 2.0
fric_a = 0.5
highest = lax.Precision.HIGHEST

def inverse_sinh(value):
    magnitude = jnp.abs(value)
    squared = magnitude * magnitude
    positive = jnp.log1p(magnitude + squared / (1.0 + jnp.sqrt(1.0 + squared)))
    return jnp.where(value < 0.0, -positive, positive)

def small_apply(mats, values):
    total = mats[:, 0, None, :] * values[0][None, :, :]
    for inner in range(1, QUANT):
        total = total + mats[:, inner, None, :] * values[inner][None, :, :]
    return total

def face_apply(mats, values):
    total = jnp.transpose(mats[:, :, 0, :], (1, 0, 2))[:, None, :, :] * values[0][None, :, :, :]
    for inner in range(1, QUANT):
        total = total + jnp.transpose(mats[:, :, inner, :], (1, 0, 2))[:, None, :, :] * values[inner][None, :, :, :]
    return total

def predict(dofs_block, star_block, kxi):
    elem_count = dofs_block.shape[1]
    derivative = dofs_block.reshape(QUANT, BASIS, elem_count)
    star_mats = star_block.reshape(3, QUANT, QUANT, elem_count)
    factor = time_step
    integral = factor * derivative
    for order_k in range(1, ORDER):
        summed = jnp.zeros_like(derivative)
        for axis_dir in range(3):
            advected = jnp.einsum('qbe,bc->qce', derivative, kxi[axis_dir], precision=highest)
            summed = summed + small_apply(star_mats[axis_dir], advected)
        derivative = summed
        factor = factor * time_step / (order_k + 1)
        integral = integral + factor * derivative
    return integral

def volume_term(integral, star_block, kxi):
    elem_count = integral.shape[2]
    star_mats = star_block.reshape(3, QUANT, QUANT, elem_count)
    summed = jnp.zeros_like(integral)
    for axis_dir in range(3):
        turned = jnp.einsum('qbe,cb->qce', integral, kxi[axis_dir], precision=highest)
        summed = summed + small_apply(star_mats[axis_dir], turned)
    return summed

def surface_terms(traces, ghost_traces, flux_block, neighbour_b, code_b, face_lift, orient):
    elem_count = traces.shape[3]
    trace_table = jnp.concatenate([traces.reshape(QUANT, FACE_BASIS, 4 * elem_count), ghost_traces], axis=2)
    neighbour_vals = jnp.take(trace_table, neighbour_b.reshape(-1), axis=2).reshape(QUANT, FACE_BASIS, 4, elem_count)
    oriented = jnp.zeros_like(neighbour_vals)
    for turn in range(3):
        rotated = jnp.einsum('qgfe,gk->qkfe', neighbour_vals, orient[turn], precision=highest)
        oriented = jnp.where(code_b == turn, rotated, oriented)
    flux_view = flux_block.reshape(4, 2, QUANT, QUANT, elem_count)
    own_part = face_apply(flux_view[:, 0], traces)
    other_part = face_apply(flux_view[:, 1], oriented)
    flux_term = jnp.einsum('pgfe,fgb->pbe', own_part + other_part, face_lift, precision=highest)
    shear = 0.5 * (traces[3] + oriented[3]) + 0.5 * (traces[6] - oriented[6])
    normal = 0.5 * (traces[0] + oriented[0])
    fault_vals = jnp.stack([shear, normal]).reshape(2, FACE_BASIS, 4 * elem_count)
    return (flux_term, fault_vals)

def friction_solve(shear, normal, shear_init, normal_init, state_var, slip_prev):
    shear_total = shear_init + shear
    normal_eff = normal_init * (1.0 + 0.5 * jnp.tanh(normal))
    growth = jnp.exp(state_var / fric_a) * 0.5
    slip_now = slip_prev
    for newton_step in range(NEWTON_ITERS):
        scaled = growth * slip_now
        misfit = shear_total - slip_now - fric_a * normal_eff * inverse_sinh(scaled)
        slope_val = -1.0 - fric_a * normal_eff * growth / jnp.sqrt(1.0 + scaled * scaled)
        slip_now = slip_now - misfit / slope_val
    return slip_now

def reference(dofs, star, flux_mats, kxi, face_proj, face_lift, orient, neighbour, orient_code, send_list, fault_part, fault_item, shear_init, normal_init, state_var, slip_prev):
    devices = N_ROW * N_COL

    def blocks(array):
        return array.reshape(array.shape[0], devices, array.shape[1] // devices).transpose(1, 0, 2)
    integral_all = lax.map(lambda pair: predict(pair[0], pair[1], kxi), (blocks(dofs), blocks(star)))
    flat_all = integral_all.reshape(devices, QUANT * BASIS, ELEM_DEV)
    sent_rows = jax.vmap(lambda rows, picks: jnp.take(rows, picks, axis=1))(flat_all, blocks(send_list))
    by_grid = sent_rows.reshape(N_ROW, N_COL, QUANT * BASIS, 4, GHOSTS)
    empty_row = jnp.zeros((1, N_COL, QUANT * BASIS, GHOSTS), by_grid.dtype)
    empty_col = jnp.zeros((N_ROW, 1, QUANT * BASIS, GHOSTS), by_grid.dtype)
    from_lower_row = jnp.concatenate([empty_row, by_grid[:-1, :, :, 0]], axis=0)
    from_upper_row = jnp.concatenate([by_grid[1:, :, :, 1], empty_row], axis=0)
    from_lower_col = jnp.concatenate([empty_col, by_grid[:, :-1, :, 2]], axis=1)
    from_upper_col = jnp.concatenate([by_grid[:, 1:, :, 3], empty_col], axis=1)
    ghost_all = jnp.concatenate([from_lower_row, from_upper_row, from_lower_col, from_upper_col], axis=3)
    ghost_all = ghost_all.reshape(devices, QUANT, BASIS, 4 * GHOSTS)

    def local_step(pack):
        dofs_block, star_block, flux_block, neighbour_b, code_b, integral, ghost_elems = pack
        traces = jnp.einsum('qbe,jbf->qfje', integral, face_proj, precision=highest)
        ghost_traces = jnp.einsum('qbg,jbf->qfjg', ghost_elems, face_proj, precision=highest)
        ghost_traces = ghost_traces.reshape(QUANT, FACE_BASIS, 16 * GHOSTS)
        flux_term, fault_vals = surface_terms(traces, ghost_traces, flux_block, neighbour_b, code_b, face_lift, orient)
        updated = dofs_block.reshape(QUANT, BASIS, ELEM_DEV) + 0.25 * (volume_term(integral, star_block, kxi) + flux_term)
        return (updated, fault_vals)
    updated_all, fault_all = lax.map(local_step, (blocks(dofs), blocks(star), blocks(flux_mats), blocks(neighbour), blocks(orient_code), integral_all, ghost_all))
    host_part = fault_part[:, 0]
    face_of = fault_item // ELEM_DEV
    elem_of = fault_item % ELEM_DEV
    fault_table = fault_all.transpose(1, 2, 0, 3).reshape(2, FACE_BASIS, devices * 4 * ELEM_DEV)
    own_vals = jnp.take(fault_table, host_part * (4 * ELEM_DEV) + fault_item, axis=2)
    slip_rate = friction_solve(own_vals[0], own_vals[1], shear_init, normal_init, state_var, slip_prev)
    lifted_all = jnp.einsum('gs,jgb->jbs', slip_rate, face_lift, precision=highest)
    lifted = jnp.zeros_like(lifted_all[0])
    for face_idx in range(4):
        lifted = jnp.where(face_of[None, :] == face_idx, lifted_all[face_idx], lifted)
    fault_push = jnp.zeros((BASIS, ELEMENTS), lifted.dtype).at[:, host_part * ELEM_DEV + elem_of].add(lifted)
    updated = updated_all.transpose(1, 2, 0, 3).reshape(QUANT, BASIS, ELEMENTS)
    updated = updated.at[3].add(-0.5 * fault_push).at[6].add(0.5 * fault_push)
    return (updated.reshape(QUANT * BASIS, ELEMENTS), slip_rate)
```

```python
import jax
import jax.numpy as jnp
from jax import lax
from jax.experimental import pallas as pl
from jax.experimental.pallas import tpu as pltpu
from jax.sharding import PartitionSpec as P

QUANT = 9
ORDER = 6
NEWTON_ITERS = 3
FACES = 4
DIMS = 3
TURNS = 3

time_step = 2.0
fric_a = 0.5
f32 = jnp.float32
half = jnp.bfloat16
MIB = 2**20
LANES = 128
SUB = 8


def up(count, unit):
    return -(-count // unit) * unit


def inverse_sinh(value):
    magnitude = jnp.abs(value)
    squared = magnitude * magnitude
    positive = jnp.log1p(magnitude + squared / (1.0 + jnp.sqrt(1.0 + squared)))
    return jnp.where(value < 0.0, -positive, positive)


def friction_solve(shear, normal, shear_init, normal_init, state_var, slip_prev):
    shear_total = shear_init + shear
    normal_eff = normal_init * (1.0 + 0.5 * jnp.tanh(normal))
    growth = jnp.exp(state_var / fric_a) * 0.5
    slip_now = slip_prev
    for newton_step in range(NEWTON_ITERS):
        scaled = growth * slip_now
        misfit = shear_total - slip_now - fric_a * normal_eff * inverse_sinh(scaled)
        slope_val = -1.0 - fric_a * normal_eff * growth / jnp.sqrt(1.0 + scaled * scaled)
        slip_now = slip_now - misfit / slope_val
    return slip_now


def split(values):
    head = values.astype(half).astype(f32)
    return head, values - head


def pad_rows(values, rows):
    if values.shape[0] == rows:
        return values
    return jnp.concatenate(
        [values, jnp.zeros((rows - values.shape[0], values.shape[1]), f32)], axis=0
    )


def pad_lanes(values, lanes):
    if values.shape[1] == lanes:
        return values
    return jnp.concatenate(
        [values, jnp.zeros((values.shape[0], lanes - values.shape[1]), f32)], axis=1
    )


def pieces(values):
    head, rest = split(values)
    return pad_rows(jnp.concatenate([head, rest, head], axis=0), up(3 * values.shape[0], 16)).astype(
        half
    )


def table(values):
    head, rest = split(values)
    return pad_lanes(
        jnp.concatenate([head, head, rest], axis=1), up(3 * values.shape[1], 16)
    ).astype(half)


def product(left, right):
    return jnp.dot(left, right, preferred_element_type=f32)


def lane_row(ref, row, side):
    return ref[row : row + 1, side * LANES : (side + 1) * LANES]


def one_hot(first, rows, index_row):
    places = lax.broadcasted_iota(jnp.int32, (rows, index_row.shape[1]), 0) + first
    return jnp.where(places == index_row, 1.0, 0.0).astype(half)


def flat_row(ref):
    return jnp.concatenate([ref[i : i + 1, :] for i in range(ref.shape[0])], axis=1)


def star_apply(star_ref, moved_ref, basis, side, emit):
    group = 3
    for first in range(0, QUANT, group):
        totals = [None] * group
        for inner in range(QUANT):
            for axis_dir in range(DIMS):
                part = moved_ref[
                    inner,
                    axis_dir * basis : (axis_dir + 1) * basis,
                    side * LANES : (side + 1) * LANES,
                ]
                for i in range(group):
                    at = (axis_dir * QUANT + first + i) * QUANT + inner
                    term = lane_row(star_ref, at, side) * part
                    totals[i] = term if totals[i] is None else totals[i] + term
        for i in range(group):
            emit(first + i, totals[i])


def flux_apply(flux_ref, which, values_of, face, side, totals):
    for inner in range(QUANT):
        value = values_of(inner)
        for p in range(QUANT):
            at = ((face * 2 + which) * QUANT + p) * QUANT + inner
            term = lane_row(flux_ref, at, side) * value
            totals[p] = term if totals[p] is None else totals[p] + term
    return totals


def cost(flops, moved):
    return pl.CostEstimate(flops=flops, bytes_accessed=moved, transcendentals=0)


def call(kernel, name, outs, scratch=(), flops=0, moved=0):
    return pl.pallas_call(
        kernel,
        name=name,
        out_shape=outs,
        scratch_shapes=list(scratch),
        cost_estimate=cost(flops, moved),
        compiler_params=pltpu.CompilerParams(vmem_limit_bytes=48 * MIB),
    )


def per_device(
    dofs,
    star,
    flux_mats,
    kxi,
    face_proj,
    face_lift,
    orient,
    neighbour,
    orient_code,
    send_list,
    fault_part,
    fault_item,
    shear_init,
    normal_init,
    state_var,
    slip_prev,
):
    basis = kxi.shape[1]
    nodes = face_proj.shape[2]
    elems = dofs.shape[1]
    sides = elems // LANES
    ghosts = send_list.shape[1]
    ghost_all = 4 * ghosts
    node_pad = up(nodes, SUB)
    faults = fault_item.shape[0]
    devices = lax.axis_size("row") * lax.axis_size("col")
    slot_most = max(2, 2 * faults // devices)
    slots = devices * slot_most
    sides_all = FACES * elems
    left_q = (QUANT + 1) // 2
    depth = up(3 * basis, 16)
    turn_depth = up(3 * node_pad, 16)
    item_row = 4 * node_pad
    fault_rows = item_row + SUB

    def slot_kernel(part_ref, item_ref, shear_ref, normal_ref, state_ref, slip_ref, out_ref, slot_ref):
        by_row = lax.broadcasted_iota(jnp.int32, (faults, faults), 0)
        by_lane = lax.broadcasted_iota(jnp.int32, (faults, faults), 1)
        down = jnp.broadcast_to(part_ref[...], (faults, faults))
        across = jnp.sum(jnp.where(by_row == by_lane, down, 0), axis=0, keepdims=True)
        rank = jnp.sum(
            jnp.where((down == across) & (by_row < by_lane), 1, 0), axis=0, keepdims=True
        )
        place = across * slot_most + rank
        slot_ref[...] = place
        chosen = one_hot(0, slots, place)
        rows = [
            pad_rows(ref[...], node_pad) for ref in (shear_ref, normal_ref, state_ref, slip_ref)
        ]
        rows.append(pad_rows((item_ref[...] + 1).astype(f32), LANES - item_row))
        head, rest = split(jnp.concatenate(rows, axis=0))
        out_ref[...] = lax.dot_general(
            jnp.concatenate([chosen, chosen], axis=1),
            jnp.concatenate([head, rest], axis=1).astype(half),
            (((1,), (1,)), ((), ())),
            preferred_element_type=f32,
        )

    def predict_kernel(dofs_ref, star_ref, kxi_ref, send_ref, out_ref, *rest):
        sends, (moved_ref, piece_ref, table_ref) = rest[:4], rest[4:]
        table_ref[...] = table(jnp.concatenate([kxi_ref[d].T for d in range(DIMS)], axis=0))
        for q in range(QUANT):
            start = dofs_ref[q * basis : (q + 1) * basis, :]
            out_ref[q * basis : (q + 1) * basis, :] = time_step * start
            piece_ref[q] = pieces(start)

        def advance(order_k, factor):
            for q in range(QUANT):
                moved_ref[q] = product(table_ref[...], piece_ref[q])
            factor = factor * time_step / (order_k + 1).astype(f32)
            for side in range(sides):
                lanes = slice(side * LANES, (side + 1) * LANES)

                def emit(p, value):
                    piece_ref[p, :, lanes] = pieces(value)
                    rows = slice(p * basis, (p + 1) * basis)
                    out_ref[rows, lanes] = out_ref[rows, lanes] + factor * value

                star_apply(star_ref, moved_ref, basis, side, emit)
            return factor

        lax.fori_loop(1, ORDER, advance, f32(time_step))
        picks = send_ref[...]
        picks = jnp.concatenate([picks, picks], axis=1)
        width = 2 * ghosts
        chosen = jnp.concatenate(
            [one_hot(0, elems, picks[d : d + 1, :]) for d in range(4)], axis=1
        )
        low = lax.broadcasted_iota(jnp.int32, (basis, width), 1) < ghosts
        got = []
        for q in range(QUANT):
            head, rest_q = split(out_ref[q * basis : (q + 1) * basis, :])
            both = product(jnp.concatenate([head, rest_q], axis=0).astype(half), chosen)
            got.append(both[:basis] + both[basis:])
        for d in range(4):
            lanes = slice(d * width, (d + 1) * width)
            for q in range(left_q):
                first = got[q][:, lanes]
                second = got[q + left_q][:, lanes] if q + left_q < QUANT else first
                sends[d][q * basis : (q + 1) * basis, :] = jnp.where(low, first, second)

    def local_kernel(
        work_ref,
        dofs_ref,
        star_ref,
        flux_ref,
        kxi_ref,
        proj_ref,
        near_ref,
        base_ref,
        own_ref,
        fric_ref,
        seen_ref,
        moved_ref,
        trace_ref,
        piece_ref,
        left_ref,
        chosen_ref,
    ):
        turn_table = table(jnp.concatenate([kxi_ref[d] for d in range(DIMS)], axis=0))
        trace_table = table(
            jnp.concatenate([pad_rows(proj_ref[j].T, node_pad) for j in range(FACES)], axis=0)
        )
        both_table = jnp.concatenate([turn_table, trace_table], axis=0)
        turned = DIMS * basis
        for q in range(QUANT):
            got = product(both_table, pieces(work_ref[q * basis : (q + 1) * basis, :]))
            moved_ref[q] = got[:turned]
            trace_ref[q] = got[turned:]
            for j in range(FACES):
                head, rest = split(got[turned + j * node_pad : turned + (j + 1) * node_pad])
                left_ref[q * 2 * node_pad : (q + 1) * 2 * node_pad, j * elems : (j + 1) * elems] = (
                    jnp.concatenate([head, rest], axis=0).astype(half)
                )
        near = flat_row(near_ref)
        for j in range(FACES):
            chosen_ref[j * elems : (j + 1) * elems, :] = one_hot(j * elems, elems, near)
        seen_ref[...] = product(left_ref[...], chosen_ref[...]).astype(half)
        for j in range(FACES):
            rows = slice(j * node_pad, (j + 1) * node_pad)
            lanes = slice(j * elems, (j + 1) * elems)
            fric_ref[:node_pad, lanes] = 0.5 * (trace_ref[3, rows] + trace_ref[6, rows])
            fric_ref[node_pad:, lanes] = 0.5 * trace_ref[0, rows]
        for side in range(sides):
            lanes = slice(side * LANES, (side + 1) * LANES)

            def emit(p, value):
                rows = slice(p * basis, (p + 1) * basis)
                base_ref[rows, lanes] = dofs_ref[rows, lanes] + 0.25 * value

            star_apply(star_ref, moved_ref, basis, side, emit)
            for j in range(FACES):
                totals = flux_apply(
                    flux_ref,
                    0,
                    lambda q: trace_ref[q, j * node_pad : (j + 1) * node_pad, lanes],
                    j,
                    side,
                    [None] * QUANT,
                )
                for p in range(QUANT):
                    at = (j * QUANT + p) * node_pad
                    own_ref[at : at + node_pad, lanes] = totals[p]

    def ghost_kernel(
        got0_ref,
        got1_ref,
        got2_ref,
        got3_ref,
        proj_ref,
        orient_ref,
        near_ref,
        code_ref,
        seen_ref,
        fric_ref,
        asked_ref,
        turned_ref,
        slip_ref,
        back_ref,
        left_ref,
        chosen_ref,
    ):
        width = 2 * ghosts
        low = lax.broadcasted_iota(jnp.int32, (basis, width), 1) < ghosts
        trace_table = table(
            jnp.concatenate([pad_rows(proj_ref[j].T, node_pad) for j in range(FACES)], axis=0)
        )
        turn_table = table(
            jnp.concatenate(
                [pad_lanes(pad_rows(orient_ref[t].T, node_pad), node_pad) for t in range(TURNS)],
                axis=0,
            )
        )
        near = flat_row(near_ref)
        for j in range(FACES):
            chosen_ref[j * ghost_all : (j + 1) * ghost_all, :] = one_hot(
                sides_all + j * ghost_all, ghost_all, near
            )
        for q in range(QUANT):
            halves = []
            for first, second in ((got0_ref, got1_ref), (got2_ref, got3_ref)):
                if q < left_q:
                    rows = slice(q * basis, (q + 1) * basis)
                    a, b = first[rows, :], pltpu.roll(second[rows, :], ghosts, 1)
                else:
                    rows = slice((q - left_q) * basis, (q - left_q + 1) * basis)
                    a, b = pltpu.roll(first[rows, :], ghosts, 1), second[rows, :]
                halves.append(jnp.where(low, a, b))
            got = product(trace_table, pieces(jnp.concatenate(halves, axis=1)))
            for j in range(FACES):
                head, rest = split(got[j * node_pad : (j + 1) * node_pad])
                left_ref[
                    q * 2 * node_pad : (q + 1) * 2 * node_pad, j * ghost_all : (j + 1) * ghost_all
                ] = jnp.concatenate([head, rest], axis=0).astype(half)
        found = product(left_ref[...], chosen_ref[...]) + seen_ref[...].astype(f32)
        code = flat_row(code_ref)
        is_zero = jnp.broadcast_to(code, (node_pad, sides_all)) == 0
        is_one = jnp.broadcast_to(code, (node_pad, sides_all)) == 1
        kept = {}
        for q in range(QUANT):
            pair = found[q * 2 * node_pad : (q + 1) * 2 * node_pad]
            right = pad_rows(jnp.concatenate([pair, pair[:node_pad]], axis=0), turn_depth)
            rotated = product(turn_table, right.astype(half))
            value = jnp.where(
                is_zero,
                rotated[:node_pad],
                jnp.where(is_one, rotated[node_pad : 2 * node_pad], rotated[2 * node_pad :]),
            )
            turned_ref[q * node_pad : (q + 1) * node_pad, :] = value
            if q in (0, 3, 6):
                kept[q] = value
        shear = fric_ref[:node_pad, :] + 0.5 * (kept[3] - kept[6])
        normal = fric_ref[node_pad:, :] + 0.5 * kept[0]
        asked = asked_ref[...].T
        item = asked[item_row : item_row + 1, :].astype(jnp.int32) - 1
        wanted = one_hot(0, sides_all, item)
        shear_head, shear_rest = split(shear)
        normal_head, normal_rest = split(normal)
        taken = product(
            jnp.concatenate([shear_head, shear_rest, normal_head, normal_rest], axis=0).astype(half),
            wanted,
        )
        own = [asked[i * node_pad : (i + 1) * node_pad] for i in range(4)]
        slip = friction_solve(
            taken[:node_pad] + taken[node_pad : 2 * node_pad],
            taken[2 * node_pad : 3 * node_pad] + taken[3 * node_pad :],
            *own,
        )
        slip_ref[...] = slip
        back_ref[...] = pad_rows(slip, LANES).T

    def final_kernel(
        turned_ref, flux_ref, own_ref, base_ref, slip_ref, asked_ref, lift_ref, out_ref, mixed_ref
    ):
        lift_table = jnp.concatenate(
            [table(pad_lanes(lift_ref[j].T, node_pad)) for j in range(FACES)], axis=1
        )
        asked = asked_ref[...].T
        item = asked[item_row : item_row + 1, :].astype(jnp.int32) - 1
        wanted = one_hot(0, sides_all, item)
        slip_head, slip_rest = split(slip_ref[...])
        pushed = lax.dot_general(
            jnp.concatenate([slip_head, slip_rest], axis=0).astype(half),
            wanted,
            (((1,), (1,)), ((), ())),
            preferred_element_type=f32,
        )
        pushed = 2.0 * (pushed[:node_pad] + pushed[node_pad:])
        for side in range(sides):
            lanes = slice(side * LANES, (side + 1) * LANES)
            for j in range(FACES):
                at = j * elems + side * LANES
                rows_of = lambda p: slice((j * QUANT + p) * node_pad, (j * QUANT + p + 1) * node_pad)
                totals = [own_ref[rows_of(p), lanes] for p in range(QUANT)]
                push = pushed[:, at : at + LANES]
                totals[3] = totals[3] - push
                totals[6] = totals[6] + push
                totals = flux_apply(
                    flux_ref,
                    1,
                    lambda q: turned_ref[q * node_pad : (q + 1) * node_pad, at : at + LANES],
                    j,
                    side,
                    totals,
                )
                for p in range(QUANT):
                    mixed_ref[p, j * turn_depth : (j + 1) * turn_depth, lanes] = pieces(totals[p])
        for p in range(QUANT):
            rows = slice(p * basis, (p + 1) * basis)
            out_ref[rows, :] = base_ref[rows, :] + 0.25 * product(lift_table, mixed_ref[p])

    def return_kernel(slot_ref, back_ref, out_ref):
        chosen = one_hot(0, slots, slot_ref[...])
        head, rest = split(back_ref[...].T[:node_pad])
        got = product(jnp.concatenate([head, rest], axis=0).astype(half), chosen)
        out_ref[...] = (got[:node_pad] + got[node_pad:])[:nodes]

    shape = jax.ShapeDtypeStruct
    work_shape = shape(dofs.shape, f32)
    asked, slot_of = call(
        slot_kernel,
        "fault_slots",
        (shape((slots, LANES), f32), shape((1, faults), jnp.int32)),
        flops=2 * slots * 2 * faults * LANES,
        moved=400_000,
    )(fault_part, fault_item.reshape(1, faults), shear_init, normal_init, state_var, slip_prev)
    asked = lax.all_to_all(
        asked.reshape(devices, slot_most, LANES), ("row", "col"), split_axis=0, concat_axis=0, tiled=True
    ).reshape(slots, LANES)

    send_shape = shape((left_q * basis, 2 * ghosts), f32)
    work, *sends = call(
        predict_kernel,
        "predict",
        (work_shape,) + (send_shape,) * 4,
        scratch=(
            pltpu.VMEM((QUANT, DIMS * basis, elems), f32),
            pltpu.VMEM((QUANT, depth, elems), half),
            pltpu.VMEM((DIMS * basis, depth), half),
        ),
        flops=5 * 2 * DIMS * basis * depth * QUANT * elems,
        moved=8_000_000,
    )(dofs, star, kxi, send_list)

    def shifted(values, axis, step):
        count = lax.axis_size(axis)
        pairs = [(i, i + step) for i in range(count) if 0 <= i + step < count]
        return lax.ppermute(values, axis, pairs)

    from_low_row = shifted(sends[0], "row", 1)
    from_high_row = shifted(sends[1], "row", -1)
    from_low_col = shifted(sends[2], "col", 1)
    from_high_col = shifted(sends[3], "col", -1)

    base, own, fric, seen = call(
        local_kernel,
        "local_terms",
        (
            work_shape,
            shape((FACES * QUANT * node_pad, elems), f32),
            shape((2 * node_pad, sides_all), f32),
            shape((QUANT * 2 * node_pad, sides_all), half),
        ),
        scratch=(
            pltpu.VMEM((QUANT, DIMS * basis, elems), f32),
            pltpu.VMEM((QUANT, FACES * node_pad, elems), f32),
            pltpu.VMEM((QUANT, depth, elems), half),
            pltpu.VMEM((QUANT * 2 * node_pad, sides_all), half),
            pltpu.VMEM((sides_all, sides_all), half),
        ),
        flops=2 * QUANT * 2 * node_pad * sides_all * sides_all,
        moved=8_000_000,
    )(work, dofs, star, flux_mats, kxi, face_proj, neighbour)

    turned, slip, back = call(
        ghost_kernel,
        "ghost_terms",
        (
            shape((QUANT * node_pad, sides_all), f32),
            shape((node_pad, slots), f32),
            shape((slots, LANES), f32),
        ),
        scratch=(
            pltpu.VMEM((QUANT * 2 * node_pad, FACES * ghost_all), half),
            pltpu.VMEM((FACES * ghost_all, sides_all), half),
        ),
        flops=2 * QUANT * 2 * node_pad * sides_all * sides_all,
        moved=8_000_000,
    )(
        from_low_row,
        from_high_row,
        from_low_col,
        from_high_col,
        face_proj,
        orient,
        neighbour,
        orient_code,
        seen,
        fric,
        asked,
    )
    back = lax.all_to_all(
        back.reshape(devices, slot_most, LANES), ("row", "col"), split_axis=0, concat_axis=0, tiled=True
    ).reshape(slots, LANES)

    dofs_next = call(
        final_kernel,
        "final_terms",
        work_shape,
        scratch=(pltpu.VMEM((QUANT, FACES * turn_depth, elems), half),),
        flops=2 * QUANT * 2 * node_pad * sides_all * sides_all,
        moved=8_000_000,
    )(turned, flux_mats, own, base, slip, asked, face_lift)

    slip_rate = call(
        return_kernel,
        "fault_return",
        shape((nodes, faults), f32),
        flops=2 * 2 * node_pad * slots * faults,
        moved=200_000,
    )(slot_of, back)
    return dofs_next, slip_rate


def solution(mesh):
    across = ("row", "col")
    placed = (
        P(None, across),
        P(None, across),
        P(None, across),
        P(),
        P(),
        P(),
        P(),
        P(None, across),
        P(None, across),
        P(None, across),
        P(across, None),
        P(across),
        P(None, across),
        P(None, across),
        P(None, across),
        P(None, across),
    )
    return jax.shard_map(
        per_device,
        mesh=mesh,
        in_specs=placed,
        out_specs=(P(None, across), P(None, across)),
        check_vma=False,
    )
```

```python
import jax
import jax.numpy as jnp
from jax import lax
from jax.experimental import pallas as pl
from jax.experimental.pallas import tpu as pltpu
from jax.sharding import PartitionSpec as P

QUANT = 9
ORDER = 6
NEWTON_ITERS = 3
FACES = 4
DIMS = 3
TURNS = 3

time_step = 2.0
fric_a = 0.5
f32 = jnp.float32
half = jnp.bfloat16
MIB = 2**20
LANES = 128
SUB = 8


def up(count, unit):
    return -(-count // unit) * unit


def inverse_sinh(value):
    magnitude = jnp.abs(value)
    squared = magnitude * magnitude
    positive = jnp.log1p(magnitude + squared / (1.0 + jnp.sqrt(1.0 + squared)))
    return jnp.where(value < 0.0, -positive, positive)


def friction_solve(shear, normal, shear_init, normal_init, state_var, slip_prev):
    shear_total = shear_init + shear
    normal_eff = normal_init * (1.0 + 0.5 * jnp.tanh(normal))
    growth = jnp.exp(state_var / fric_a) * 0.5
    slip_now = slip_prev
    for newton_step in range(NEWTON_ITERS):
        scaled = growth * slip_now
        misfit = shear_total - slip_now - fric_a * normal_eff * inverse_sinh(scaled)
        slope_val = -1.0 - fric_a * normal_eff * growth / jnp.sqrt(1.0 + scaled * scaled)
        slip_now = slip_now - misfit / slope_val
    return slip_now


def split(values):
    head = values.astype(half).astype(f32)
    return head, values - head


def pad_rows(values, rows):
    if values.shape[0] == rows:
        return values
    return jnp.concatenate(
        [values, jnp.zeros((rows - values.shape[0], values.shape[1]), f32)], axis=0
    )


def pad_lanes(values, lanes):
    if values.shape[1] == lanes:
        return values
    return jnp.concatenate(
        [values, jnp.zeros((values.shape[0], lanes - values.shape[1]), f32)], axis=1
    )


def pieces(values):
    head, rest = split(values)
    return pad_rows(jnp.concatenate([head, rest, head], axis=0), up(3 * values.shape[0], 16)).astype(
        half
    )


def table(values):
    head, rest = split(values)
    return pad_lanes(
        jnp.concatenate([head, head, rest], axis=1), up(3 * values.shape[1], 16)
    ).astype(half)


def product(left, right):
    return jnp.dot(left, right, preferred_element_type=f32)


def lane_row(ref, row, side):
    return ref[row : row + 1, side * LANES : (side + 1) * LANES]


def one_hot(first, rows, index_row):
    places = lax.broadcasted_iota(jnp.int32, (rows, index_row.shape[1]), 0) + first
    return jnp.where(places == index_row, 1.0, 0.0).astype(half)


def flat_row(ref):
    return jnp.concatenate([ref[i : i + 1, :] for i in range(ref.shape[0])], axis=1)


def star_apply(star_ref, moved_ref, basis, side, emit):
    group = 3
    for first in range(0, QUANT, group):
        totals = [None] * group
        for inner in range(QUANT):
            for axis_dir in range(DIMS):
                part = moved_ref[
                    inner,
                    axis_dir * basis : (axis_dir + 1) * basis,
                    side * LANES : (side + 1) * LANES,
                ]
                for i in range(group):
                    at = (axis_dir * QUANT + first + i) * QUANT + inner
                    term = lane_row(star_ref, at, side) * part
                    totals[i] = term if totals[i] is None else totals[i] + term
        for i in range(group):
            emit(first + i, totals[i])


def flux_apply(flux_ref, which, values_of, face, side, totals):
    for inner in range(QUANT):
        value = values_of(inner)
        for p in range(QUANT):
            at = ((face * 2 + which) * QUANT + p) * QUANT + inner
            term = lane_row(flux_ref, at, side) * value
            totals[p] = term if totals[p] is None else totals[p] + term
    return totals


class Kept:
    def __init__(self, array):
        self.array = array


class Left:
    def __init__(self, array):
        self.array = array


class Inputs:
    def __init__(self, sources, targets, sems):
        self.sources, self.targets, self.waiting = sources, targets, {}
        for i, (source, target) in enumerate(zip(sources, targets)):
            if source is target:
                continue
            self.waiting[i] = pltpu.make_async_copy(source, target, sems.at[i])
            self.waiting[i].start()

    def __getitem__(self, i):
        if i in self.waiting:
            self.waiting.pop(i).wait()
        return self.targets[i]

    def rest(self):
        for move in self.waiting.values():
            move.wait()


class Outputs:
    def __init__(self, targets, sources, sems):
        self.targets, self.sources, self.sems = targets, sources, sems
        self.moving = []

    def __getitem__(self, i):
        return self.targets[i] if self.sources[i] is None else self.sources[i]

    def flush(self, i, rows=None):
        source, target = self.sources[i], self.targets[i]
        if source is None:
            return
        if rows is not None:
            source, target = source.at[rows], target.at[rows]
        move = pltpu.make_async_copy(source, target, self.sems.at[len(self.moving)])
        move.start()
        self.moving.append(move)

    def wait(self):
        for move in self.moving:
            move.wait()


def call(kernel, name, ins, outs, scratch=(), flops=0, moved=0, room=32, flushes=None):
    n_in, n_out = len(ins), len(outs)
    placed = [i for i, one in enumerate(outs) if one[2] == "hbm"]
    stays = [isinstance(one, Kept) for one in ins]
    brought = [i for i in range(n_in) if not isinstance(ins[i], (Kept, Left))]
    ins = [one.array if isinstance(one, (Kept, Left)) else one for one in ins]
    flushes = flushes or max(1, len(placed))

    def body(*refs):
        sources, targets = refs[:n_in], refs[n_in : n_in + n_out]
        at = n_in + n_out
        held = list(sources)
        for i in brought:
            held[i], at = refs[at], at + 1
        kept, at = refs[at : at + len(placed)], at + len(placed)
        in_sems, out_sems, *more = refs[at:]
        source_of = [None] * n_out
        for i, ref in zip(placed, kept):
            source_of[i] = ref
        inputs = Inputs(sources, held, in_sems)
        outputs = Outputs(targets, source_of, out_sems)
        kernel(inputs, outputs, *more)
        inputs.rest()
        outputs.wait()

    shapes = [
        {"hbm": pltpu.HBM, "vmem": pltpu.VMEM, "any": jax.ShapeDtypeStruct}[one[2]](one[0], one[1])
        for one in outs
    ]
    spaces = [pltpu.VMEM if one else pltpu.HBM for one in stays]
    return pl.pallas_call(
        body,
        name=name,
        out_shape=shapes,
        in_specs=[pl.BlockSpec(memory_space=space) for space in spaces],
        scratch_shapes=[
            *(pltpu.VMEM(ins[i].shape, ins[i].dtype) for i in brought),
            *(pltpu.VMEM(outs[i][0], outs[i][1]) for i in placed),
            pltpu.SemaphoreType.DMA((max(1, n_in),)),
            pltpu.SemaphoreType.DMA((flushes,)),
            *scratch,
        ],
        cost_estimate=pl.CostEstimate(flops=flops, bytes_accessed=moved, transcendentals=0),
        compiler_params=pltpu.CompilerParams(vmem_limit_bytes=room * MIB),
    )(*(pltpu.with_memory_space_constraint(a, space) for a, space in zip(ins, spaces)))


def per_device(
    dofs,
    star,
    flux_mats,
    kxi,
    face_proj,
    face_lift,
    orient,
    neighbour,
    orient_code,
    send_list,
    fault_part,
    fault_item,
    shear_init,
    normal_init,
    state_var,
    slip_prev,
):
    basis = kxi.shape[1]
    nodes = face_proj.shape[2]
    elems = dofs.shape[1]
    sides = elems // LANES
    ghosts = send_list.shape[1]
    ghost_all = 4 * ghosts
    node_pad = up(nodes, SUB)
    faults = fault_item.shape[0]
    devices = lax.axis_size("row") * lax.axis_size("col")
    slot_most = max(2, 2 * faults // devices)
    slots = devices * slot_most
    sides_all = FACES * elems
    left_q = (QUANT + 1) // 2
    depth = up(3 * basis, 16)
    turn_depth = up(3 * node_pad, 16)
    item_row = 4 * node_pad
    pair = 2 * node_pad
    first_q = (0, 3, 6)
    rest_q = tuple(q for q in range(QUANT) if q not in first_q)

    def odd_place():
        return lax.axis_index("row") % 2 == 1, lax.axis_index("col") % 2 == 1

    def predict_kernel(ins, outs, moved_ref, piece_ref, table_ref, star_sem):
        kxi_at, part_at, item_at, fault_at, dofs_at, star_at, send_at = 0, 1, 2, 3, 7, 8, 9
        proj_at, orient_at, lift_at, near_at, code_at = range(10, 15)
        asked_at, slot_at, work_at, sends_at = 0, 1, 2, 3
        back_table_at, trace_table_at, turn_table_at, lift_table_at = range(7, 11)
        near_out, code_out, star_out = range(11, 14)
        star_move = pltpu.make_async_copy(ins.sources[star_at], outs[star_out], star_sem)
        star_move.start()
        kxi_ref = ins[kxi_at]
        table_ref[...] = table(jnp.concatenate([kxi_ref[d].T for d in range(DIMS)], axis=0))
        by_row = lax.broadcasted_iota(jnp.int32, (faults, faults), 0)
        by_lane = lax.broadcasted_iota(jnp.int32, (faults, faults), 1)
        across = ins[part_at][...]
        wide = jnp.broadcast_to(across, (faults, faults))
        down = jnp.sum(jnp.where(by_row == by_lane, wide, 0), axis=1, keepdims=True)
        rank = jnp.sum(
            jnp.where((down == across) & (by_row < by_lane), 1, 0), axis=0, keepdims=True
        )
        place = across * slot_most + rank
        outs[slot_at][...] = place
        outs.flush(slot_at)
        chosen = one_hot(0, slots, place)
        item = (ins[item_at][...] + 1).astype(f32)
        rows = [pad_rows(ins[fault_at + i][...], node_pad) for i in range(4)]
        rows.append(pad_rows(item, LANES - item_row))
        head, rest = split(jnp.concatenate(rows, axis=0))
        outs[asked_at][...] = lax.dot_general(
            jnp.concatenate([chosen, chosen], axis=1),
            jnp.concatenate([head, rest], axis=1).astype(half),
            (((1,), (1,)), ((), ())),
            preferred_element_type=f32,
        )
        outs.flush(asked_at)

        proj_ref, orient_ref, lift_ref = ins[proj_at], ins[orient_at], ins[lift_at]
        outs[back_table_at][...] = table(
            jnp.concatenate([kxi_ref[d] for d in range(DIMS)], axis=0)
        )
        outs[trace_table_at][...] = table(
            jnp.concatenate([pad_rows(proj_ref[:, j, :], node_pad) for j in range(FACES)], axis=0)
        )
        outs[turn_table_at][...] = table(
            jnp.concatenate(
                [pad_lanes(pad_rows(orient_ref[t].T, node_pad), node_pad) for t in range(TURNS)],
                axis=0,
            )
        )
        outs[lift_table_at][...] = jnp.concatenate(
            [table(pad_lanes(lift_ref[:, j, :].T, node_pad)) for j in range(FACES)], axis=1
        )
        outs.flush(lift_table_at)
        odd_row, odd_col = odd_place()
        near = flat_row(ins[near_at])
        block = (near // ghosts) % 4
        flip = jnp.where(block < 2, jnp.where(odd_row, 0, 1), jnp.where(odd_col, 0, 1))
        outs[near_out][...] = jnp.where(
            near < sides_all, near, near + ghosts * flip * (1 - 2 * (block % 2))
        )
        outs[code_out][...] = flat_row(ins[code_at])

        dofs_ref, work_ref = ins[dofs_at], outs[work_at]
        for q in range(QUANT):
            start = dofs_ref[q * basis : (q + 1) * basis, :]
            work_ref[q * basis : (q + 1) * basis, :] = time_step * start
            piece_ref[q] = pieces(start)
        star_ref = outs[star_out]
        star_move.wait()

        def advance(order_k, factor):
            for q in range(QUANT):
                moved_ref[q] = product(table_ref[...], piece_ref[q])
            factor = factor * time_step / (order_k + 1).astype(f32)
            for side in range(sides):
                lanes = slice(side * LANES, (side + 1) * LANES)

                def emit(p, value):
                    piece_ref[p, :, lanes] = pieces(value)
                    rows = slice(p * basis, (p + 1) * basis)
                    work_ref[rows, lanes] = work_ref[rows, lanes] + factor * value

                star_apply(star_ref, moved_ref, basis, side, emit)
            return factor

        lax.fori_loop(1, ORDER, advance, f32(time_step))
        outs.flush(work_at)
        picks = ins[send_at][...]
        picks = jnp.concatenate([picks, picks], axis=1)
        order = [
            jnp.where(odd_row, picks[1:2], picks[0:1]),
            jnp.where(odd_row, picks[0:1], picks[1:2]),
            jnp.where(odd_col, picks[3:4], picks[2:3]),
            jnp.where(odd_col, picks[2:3], picks[3:4]),
        ]
        width = 2 * ghosts
        chosen = jnp.concatenate([one_hot(0, elems, order[d]) for d in range(4)], axis=1)
        low = lax.broadcasted_iota(jnp.int32, (basis, width), 1) < ghosts
        got = []
        for q in range(QUANT):
            head, rest = split(work_ref[q * basis : (q + 1) * basis, :])
            both = product(jnp.concatenate([head, rest], axis=0).astype(half), chosen)
            got.append(both[:basis] + both[basis:])
        for d in range(4):
            lanes = slice(d * width, (d + 1) * width)
            for q in range(left_q):
                first = got[q][:, lanes]
                second = got[q + left_q][:, lanes] if q + left_q < QUANT else first
                outs[sends_at + d][q * basis : (q + 1) * basis, :] = jnp.where(low, first, second)

    def local_kernel(ins, outs, moved_ref, trace_ref, left_ref, chosen_ref):
        near_at, back_table_at, trace_table_at, work_at, star_at, flux_at = range(6)
        seen_at, fric_at, volume_at, own_at = range(4)
        back_table, trace_table = ins[back_table_at][...], ins[trace_table_at][...]
        work_ref = ins[work_at]
        for q in range(QUANT):
            right = pieces(work_ref[q * basis : (q + 1) * basis, :])
            moved_ref[q] = product(back_table, right)
            got = product(trace_table, right)
            trace_ref[q] = got
            for j in range(FACES):
                head, rest = split(got[j * node_pad : (j + 1) * node_pad])
                left_ref[q * pair : (q + 1) * pair, j * elems : (j + 1) * elems] = jnp.concatenate(
                    [head, rest], axis=0
                ).astype(half)
        star_ref, volume_ref = ins[star_at], outs[volume_at]
        for side in range(sides):
            lanes = slice(side * LANES, (side + 1) * LANES)

            def emit(p, value):
                volume_ref[p * basis : (p + 1) * basis, lanes] = value

            star_apply(star_ref, moved_ref, basis, side, emit)
        outs.flush(volume_at)
        flux_ref, own_ref = ins[flux_at], outs[own_at]
        for side in range(sides):
            lanes = slice(side * LANES, (side + 1) * LANES)
            for j in range(FACES):
                totals = flux_apply(
                    flux_ref,
                    0,
                    lambda q: trace_ref[q, j * node_pad : (j + 1) * node_pad, lanes],
                    j,
                    side,
                    [None] * QUANT,
                )
                for p in range(QUANT):
                    at = (j * QUANT + p) * node_pad
                    own_ref[at : at + node_pad, lanes] = totals[p]
        outs.flush(own_at)
        near = ins[near_at][...]
        for j in range(FACES):
            chosen_ref[j * elems : (j + 1) * elems, :] = one_hot(j * elems, elems, near)
        outs[seen_at][...] = product(left_ref[...], chosen_ref[...]).astype(half)
        fric_ref = outs[fric_at]
        for j in range(FACES):
            rows = slice(j * node_pad, (j + 1) * node_pad)
            lanes = slice(j * elems, (j + 1) * elems)
            fric_ref[:node_pad, lanes] = 0.5 * (trace_ref[3, rows] + trace_ref[6, rows])
            fric_ref[node_pad:, lanes] = 0.5 * trace_ref[0, rows]

    def seen_across(
        got_refs, quants, trace_table, turn_table, near, code, seen_ref, chosen_ref, left_ref, emit
    ):
        low = lax.broadcasted_iota(jnp.int32, (basis, 2 * ghosts), 1) < ghosts
        for j in range(FACES):
            chosen_ref[j * ghost_all : (j + 1) * ghost_all, :] = one_hot(
                sides_all + j * ghost_all, ghost_all, near
            )
        for at, q in enumerate(quants):
            halves = []
            for first, second in (got_refs[:2], got_refs[2:]):
                if q < left_q:
                    rows = slice(q * basis, (q + 1) * basis)
                    a, b = first[rows, :], pltpu.roll(second[rows, :], ghosts, 1)
                else:
                    rows = slice((q - left_q) * basis, (q - left_q + 1) * basis)
                    a, b = pltpu.roll(first[rows, :], ghosts, 1), second[rows, :]
                halves.append(jnp.where(low, a, b))
            got = product(trace_table, pieces(jnp.concatenate(halves, axis=1)))
            for j in range(FACES):
                head, rest = split(got[j * node_pad : (j + 1) * node_pad])
                left_ref[
                    at * pair : (at + 1) * pair, j * ghost_all : (j + 1) * ghost_all
                ] = jnp.concatenate([head, rest], axis=0).astype(half)
        found = product(left_ref[...], chosen_ref[...])
        is_zero = jnp.broadcast_to(code, (node_pad, sides_all)) == 0
        is_one = jnp.broadcast_to(code, (node_pad, sides_all)) == 1
        for at, q in enumerate(quants):
            both = found[at * pair : (at + 1) * pair]
            both = both + seen_ref[q * pair : (q + 1) * pair].astype(f32)
            right = pad_rows(jnp.concatenate([both, both[:node_pad]], axis=0), turn_depth)
            rotated = product(turn_table, right.astype(half))
            emit(
                q,
                jnp.where(
                    is_zero,
                    rotated[:node_pad],
                    jnp.where(is_one, rotated[node_pad : 2 * node_pad], rotated[2 * node_pad :]),
                ),
            )

    def friction_kernel(ins, outs, chosen_ref, left_ref):
        got_at = range(4)
        trace_table_at, turn_table_at, near_at, code_at, seen_at, fric_at, asked_at = range(4, 11)
        back_at, turned_at, slip_at = range(3)
        kept = {}

        def emit(q, value):
            kept[q] = value
            at = first_q.index(q)
            outs[turned_at][at * node_pad : (at + 1) * node_pad, :] = value

        seen_across(
            [ins[i] for i in got_at],
            first_q,
            ins[trace_table_at][...],
            ins[turn_table_at][...],
            ins[near_at][...],
            ins[code_at][...],
            ins[seen_at],
            chosen_ref,
            left_ref,
            emit,
        )
        outs.flush(turned_at)
        fric_ref = ins[fric_at]
        shear = fric_ref[:node_pad, :] + 0.5 * (kept[3] - kept[6])
        normal = fric_ref[node_pad:, :] + 0.5 * kept[0]
        asked = ins[asked_at][...].T
        item = asked[item_row : item_row + 1, :].astype(jnp.int32) - 1
        wanted = one_hot(0, sides_all, item)
        shear_head, shear_rest = split(shear)
        normal_head, normal_rest = split(normal)
        taken = product(
            jnp.concatenate([shear_head, shear_rest, normal_head, normal_rest], axis=0).astype(half),
            wanted,
        )
        own = [asked[i * node_pad : (i + 1) * node_pad] for i in range(4)]
        slip = friction_solve(
            taken[:node_pad] + taken[node_pad : 2 * node_pad],
            taken[2 * node_pad : 3 * node_pad] + taken[3 * node_pad :],
            *own,
        )
        outs[back_at][...] = pad_rows(slip, LANES).T
        outs[slip_at][...] = slip
        outs.flush(slip_at)

    def final_kernel(ins, outs, turned_ref, mixed_ref, chosen_ref, left_ref):
        got_at = range(4)
        trace_table_at, turn_table_at, near_at, code_at, seen_at, asked_at, slip_at = range(4, 11)
        first_at, flux_at, own_at, lift_table_at, volume_at, dofs_at = range(11, 17)

        def emit(q, value):
            turned_ref[q * node_pad : (q + 1) * node_pad, :] = value

        seen_across(
            [ins[i] for i in got_at],
            rest_q,
            ins[trace_table_at][...],
            ins[turn_table_at][...],
            ins[near_at][...],
            ins[code_at][...],
            ins[seen_at],
            chosen_ref,
            left_ref,
            emit,
        )
        for at, q in enumerate(first_q):
            emit(q, ins[first_at][at * node_pad : (at + 1) * node_pad, :])
        asked = ins[asked_at][...].T
        item = asked[item_row : item_row + 1, :].astype(jnp.int32) - 1
        wanted = one_hot(0, sides_all, item)
        slip_head, slip_rest = split(ins[slip_at][...])
        pushed = lax.dot_general(
            jnp.concatenate([slip_head, slip_rest], axis=0).astype(half),
            wanted,
            (((1,), (1,)), ((), ())),
            preferred_element_type=f32,
        )
        pushed = 2.0 * (pushed[:node_pad] + pushed[node_pad:])
        own_ref, flux_ref = ins[own_at], ins[flux_at]
        for side in range(sides):
            lanes = slice(side * LANES, (side + 1) * LANES)
            for j in range(FACES):
                at = j * elems + side * LANES
                rows_of = lambda p: slice((j * QUANT + p) * node_pad, (j * QUANT + p + 1) * node_pad)
                totals = [own_ref[rows_of(p), lanes] for p in range(QUANT)]
                push = pushed[:, at : at + LANES]
                totals[3] = totals[3] - push
                totals[6] = totals[6] + push
                totals = flux_apply(
                    flux_ref,
                    1,
                    lambda q: turned_ref[q * node_pad : (q + 1) * node_pad, at : at + LANES],
                    j,
                    side,
                    totals,
                )
                for p in range(QUANT):
                    mixed_ref[p, j * turn_depth : (j + 1) * turn_depth, lanes] = pieces(totals[p])
        lift_table, volume_ref, dofs_ref = ins[lift_table_at][...], ins[volume_at], ins[dofs_at]
        for p in range(QUANT):
            rows = slice(p * basis, (p + 1) * basis)
            lifted = volume_ref[rows, :] + product(lift_table, mixed_ref[p])
            outs[0][rows, :] = dofs_ref[rows, :] + 0.25 * lifted
            outs.flush(0, rows)

    def return_kernel(ins, outs):
        chosen = one_hot(0, slots, ins[0][...])
        head, rest = split(ins[1][...].T[:node_pad])
        got = product(jnp.concatenate([head, rest], axis=0).astype(half), chosen)
        outs[0][...] = (got[:node_pad] + got[node_pad:])[:nodes]

    vmem = pltpu.VMEM
    proj_rows = jnp.transpose(face_proj, (2, 0, 1))
    lift_rows = jnp.transpose(face_lift, (1, 0, 2))
    *first_outs, back_table, trace_table, turn_table, lift_table, near, code, star_kept = call(
        predict_kernel,
        "predict",
        [
            kxi,
            fault_part.reshape(1, faults),
            fault_item.reshape(1, faults),
            shear_init,
            normal_init,
            state_var,
            slip_prev,
            dofs,
            Left(star),
            send_list,
            proj_rows,
            orient,
            lift_rows,
            neighbour,
            orient_code,
        ],
        [
            ((slots, LANES), f32, "hbm"),
            ((1, faults), jnp.int32, "vmem"),
            (dofs.shape, f32, "vmem"),
        ]
        + [((left_q * basis, 2 * ghosts), f32, "any")] * 4
        + [
            ((DIMS * basis, depth), half, "vmem"),
            ((FACES * node_pad, depth), half, "vmem"),
            ((TURNS * node_pad, turn_depth), half, "vmem"),
            ((basis, FACES * turn_depth), half, "hbm"),
            ((1, sides_all), jnp.int32, "vmem"),
            ((1, sides_all), jnp.int32, "vmem"),
            (star.shape, f32, "vmem"),
        ],
        scratch=(
            vmem((QUANT, DIMS * basis, elems), f32),
            vmem((QUANT, depth, elems), half),
            vmem((DIMS * basis, depth), half),
            pltpu.SemaphoreType.DMA,
        ),
        flops=5 * 2 * DIMS * basis * depth * QUANT * elems,
        moved=8_000_000,
    )

    asked, slot_of, work, *sends = first_outs
    asked = lax.all_to_all(
        asked.reshape(devices, slot_most, LANES), ("row", "col"), split_axis=0, concat_axis=0, tiled=True
    ).reshape(slots, LANES)

    def swapped(values, axis, first):
        pairs = [(i, i + 1) for i in range(first, lax.axis_size(axis) - 1, 2)]
        return lax.ppermute(values, axis, pairs + [(b, a) for a, b in pairs])

    arrived = [
        swapped(sends[0], "row", 0),
        swapped(sends[1], "row", 1),
        swapped(sends[2], "col", 0),
        swapped(sends[3], "col", 1),
    ]

    seen, fric, volume, own = call(
        local_kernel,
        "local_terms",
        [*(Kept(one) for one in (near, back_table, trace_table, work, star_kept)), flux_mats],
        [
            ((QUANT * pair, sides_all), half, "vmem"),
            ((pair, sides_all), f32, "vmem"),
            (dofs.shape, f32, "hbm"),
            ((FACES * QUANT * node_pad, elems), f32, "hbm"),
        ],
        scratch=(
            vmem((QUANT, DIMS * basis, elems), f32),
            vmem((QUANT, FACES * node_pad, elems), f32),
            vmem((QUANT * pair, sides_all), half),
            vmem((sides_all, sides_all), half),
        ),
        flops=2 * QUANT * pair * sides_all * sides_all,
        moved=8_000_000,
    )

    back, first_turned, slip = call(
        friction_kernel,
        "friction",
        [Kept(one) for one in (*arrived, trace_table, turn_table, near, code, seen, fric, asked)],
        [
            ((slots, LANES), f32, "any"),
            ((len(first_q) * node_pad, sides_all), f32, "vmem"),
            ((node_pad, slots), f32, "vmem"),
        ],
        scratch=(vmem((FACES * ghost_all, sides_all), half), vmem((len(first_q) * pair, FACES * ghost_all), half),),
        flops=2 * len(first_q) * pair * sides_all * sides_all,
        moved=4_000_000,
    )
    back = lax.all_to_all(
        back.reshape(devices, slot_most, LANES), ("row", "col"), split_axis=0, concat_axis=0, tiled=True
    ).reshape(slots, LANES)

    (dofs_next,) = call(
        final_kernel,
        "final_terms",
        [
            *(Kept(one) for one in arrived),
            Kept(trace_table),
            Kept(turn_table),
            Kept(near),
            Kept(code),
            Kept(seen),
            Kept(asked),
            Kept(slip),
            Kept(first_turned),
            flux_mats,
            own,
            lift_table,
            volume,
            dofs,
        ],
        [(dofs.shape, f32, "hbm")],
        scratch=(
            vmem((QUANT * node_pad, sides_all), f32),
            vmem((QUANT, FACES * turn_depth, elems), half),
            vmem((FACES * ghost_all, sides_all), half),
            vmem((len(rest_q) * pair, FACES * ghost_all), half),
        ),
        flops=2 * QUANT * pair * sides_all * sides_all,
        moved=8_000_000,
        flushes=QUANT,
    )

    (slip_rate,) = call(
        return_kernel,
        "fault_return",
        [Kept(slot_of), Kept(back)],
        [((nodes, faults), f32, "any")],
        flops=2 * pair * slots * faults,
        moved=200_000,
    )
    return dofs_next, slip_rate


def solution(mesh):
    across = ("row", "col")
    placed = (
        P(None, across),
        P(None, across),
        P(None, across),
        P(),
        P(),
        P(),
        P(),
        P(None, across),
        P(None, across),
        P(None, across),
        P(across, None),
        P(across),
        P(None, across),
        P(None, across),
        P(None, across),
        P(None, across),
    )
    return jax.shard_map(
        per_device,
        mesh=mesh,
        in_specs=placed,
        out_specs=(P(None, across), P(None, across)),
        check_vma=False,
    )
```

```python
import jax
import jax.numpy as jnp
from jax import lax
from jax.experimental import pallas as pl
from jax.experimental.pallas import tpu as pltpu
from jax.sharding import PartitionSpec as P

QUANT = 9
ORDER = 6
NEWTON_ITERS = 3
FACES = 4
DIMS = 3
TURNS = 3

time_step = 2.0
fric_a = 0.5
f32 = jnp.float32
half = jnp.bfloat16
MIB = 2**20
LANES = 128
SUB = 8


def up(count, unit):
    return -(-count // unit) * unit


def inverse_sinh(value):
    magnitude = jnp.abs(value)
    squared = magnitude * magnitude
    positive = jnp.log1p(magnitude + squared / (1.0 + jnp.sqrt(1.0 + squared)))
    return jnp.where(value < 0.0, -positive, positive)


def friction_solve(shear, normal, shear_init, normal_init, state_var, slip_prev):
    shear_total = shear_init + shear
    normal_eff = normal_init * (1.0 + 0.5 * jnp.tanh(normal))
    growth = jnp.exp(state_var / fric_a) * 0.5
    slip_now = slip_prev
    for newton_step in range(NEWTON_ITERS):
        scaled = growth * slip_now
        misfit = shear_total - slip_now - fric_a * normal_eff * inverse_sinh(scaled)
        slope_val = -1.0 - fric_a * normal_eff * growth / jnp.sqrt(1.0 + scaled * scaled)
        slip_now = slip_now - misfit / slope_val
    return slip_now


def split(values):
    head = values.astype(half).astype(f32)
    return head, values - head


def pad_rows(values, rows):
    if values.shape[0] == rows:
        return values
    return jnp.concatenate(
        [values, jnp.zeros((rows - values.shape[0], values.shape[1]), f32)], axis=0
    )


def pad_lanes(values, lanes):
    if values.shape[1] == lanes:
        return values
    return jnp.concatenate(
        [values, jnp.zeros((values.shape[0], lanes - values.shape[1]), f32)], axis=1
    )


def pieces(values):
    head, rest = split(values)
    return pad_rows(jnp.concatenate([head, rest, head], axis=0), up(3 * values.shape[0], 16)).astype(
        half
    )


def table(values):
    head, rest = split(values)
    return pad_lanes(
        jnp.concatenate([head, head, rest], axis=1), up(3 * values.shape[1], 16)
    ).astype(half)


def product(left, right):
    return jnp.dot(left, right, preferred_element_type=f32)


def lane_row(ref, row, side):
    return ref[row : row + 1, side * LANES : (side + 1) * LANES]


def one_hot(first, rows, index_row):
    places = lax.broadcasted_iota(jnp.int32, (rows, index_row.shape[1]), 0) + first
    return jnp.where(places == index_row, 1.0, 0.0).astype(half)


def flat_row(ref):
    return jnp.concatenate([ref[i : i + 1, :] for i in range(ref.shape[0])], axis=1)


def star_apply(star_ref, moved_ref, basis, side, emit):
    group = 3
    for first in range(0, QUANT, group):
        totals = [None] * group
        for inner in range(QUANT):
            for axis_dir in range(DIMS):
                part = moved_ref[
                    inner,
                    axis_dir * basis : (axis_dir + 1) * basis,
                    side * LANES : (side + 1) * LANES,
                ]
                for i in range(group):
                    at = (axis_dir * QUANT + first + i) * QUANT + inner
                    term = lane_row(star_ref, at, side) * part
                    totals[i] = term if totals[i] is None else totals[i] + term
        for i in range(group):
            emit(first + i, totals[i])


def flux_apply(flux_ref, which, values_of, face, side, totals):
    for inner in range(QUANT):
        value = values_of(inner)
        for p in range(QUANT):
            at = ((face * 2 + which) * QUANT + p) * QUANT + inner
            term = lane_row(flux_ref, at, side) * value
            totals[p] = term if totals[p] is None else totals[p] + term
    return totals


class Kept:
    def __init__(self, array):
        self.array = array


class Inputs:
    def __init__(self, sources, targets, sems):
        self.sources, self.targets, self.waiting = sources, targets, {}
        for i, (source, target) in enumerate(zip(sources, targets)):
            if source is target:
                continue
            self.waiting[i] = pltpu.make_async_copy(source, target, sems.at[i])
            self.waiting[i].start()

    def __getitem__(self, i):
        if i in self.waiting:
            self.waiting.pop(i).wait()
        return self.targets[i]

    def rest(self):
        for move in self.waiting.values():
            move.wait()


class Outputs:
    def __init__(self, targets, sources, sems):
        self.targets, self.sources, self.sems = targets, sources, sems
        self.moving = []

    def __getitem__(self, i):
        return self.targets[i] if self.sources[i] is None else self.sources[i]

    def flush(self, i, rows=None):
        source, target = self.sources[i], self.targets[i]
        if source is None:
            return
        if rows is not None:
            source, target = source.at[rows], target.at[rows]
        move = pltpu.make_async_copy(source, target, self.sems.at[len(self.moving)])
        move.start()
        self.moving.append(move)

    def wait(self):
        for move in self.moving:
            move.wait()


def call(kernel, name, ins, outs, scratch=(), flops=0, moved=0, room=32, flushes=None):
    n_in, n_out = len(ins), len(outs)
    placed = [i for i, one in enumerate(outs) if one[2] == "hbm"]
    stays = [isinstance(one, Kept) for one in ins]
    brought = [i for i in range(n_in) if not isinstance(ins[i], Kept)]
    ins = [one.array if isinstance(one, Kept) else one for one in ins]
    flushes = flushes or max(1, len(placed))

    def body(*refs):
        sources, targets = refs[:n_in], refs[n_in : n_in + n_out]
        at = n_in + n_out
        held = list(sources)
        for i in brought:
            held[i], at = refs[at], at + 1
        kept, at = refs[at : at + len(placed)], at + len(placed)
        in_sems, out_sems, *more = refs[at:]
        source_of = [None] * n_out
        for i, ref in zip(placed, kept):
            source_of[i] = ref
        inputs = Inputs(sources, held, in_sems)
        outputs = Outputs(targets, source_of, out_sems)
        kernel(inputs, outputs, *more)
        inputs.rest()
        outputs.wait()

    shapes = [
        {"hbm": pltpu.HBM, "vmem": pltpu.VMEM, "any": jax.ShapeDtypeStruct}[one[2]](one[0], one[1])
        for one in outs
    ]
    spaces = [pltpu.VMEM if one else pltpu.HBM for one in stays]
    return pl.pallas_call(
        body,
        name=name,
        out_shape=shapes,
        in_specs=[pl.BlockSpec(memory_space=space) for space in spaces],
        scratch_shapes=[
            *(pltpu.VMEM(ins[i].shape, ins[i].dtype) for i in brought),
            *(pltpu.VMEM(outs[i][0], outs[i][1]) for i in placed),
            pltpu.SemaphoreType.DMA((max(1, n_in),)),
            pltpu.SemaphoreType.DMA((flushes,)),
            *scratch,
        ],
        cost_estimate=pl.CostEstimate(flops=flops, bytes_accessed=moved, transcendentals=0),
        compiler_params=pltpu.CompilerParams(vmem_limit_bytes=room * MIB),
    )(*(pltpu.with_memory_space_constraint(a, space) for a, space in zip(ins, spaces)))


def per_device(
    dofs,
    star,
    flux_mats,
    kxi,
    face_proj,
    face_lift,
    orient,
    neighbour,
    orient_code,
    send_list,
    fault_part,
    fault_item,
    shear_init,
    normal_init,
    state_var,
    slip_prev,
):
    basis = kxi.shape[1]
    nodes = face_proj.shape[2]
    elems = dofs.shape[1]
    sides = elems // LANES
    ghosts = send_list.shape[1]
    ghost_all = 4 * ghosts
    node_pad = up(nodes, SUB)
    faults = fault_item.shape[0]
    devices = lax.axis_size("row") * lax.axis_size("col")
    slot_most = max(2, 2 * faults // devices)
    slots = devices * slot_most
    sides_all = FACES * elems
    left_q = (QUANT + 1) // 2
    depth = up(3 * basis, 16)
    turn_depth = up(3 * node_pad, 16)
    item_row = 4 * node_pad
    pair = 2 * node_pad
    first_q = (0, 3, 6)
    slot_lanes = up(node_pad, 32)
    per_row = LANES // slot_lanes
    chunk = slot_most * slot_lanes
    chunk_shape = (chunk // LANES, LANES) if chunk % LANES == 0 else (chunk,)

    def odd_place():
        return lax.axis_index("row") % 2 == 1, lax.axis_index("col") % 2 == 1

    def predict_kernel(ins, outs, moved_ref, piece_ref, table_ref):
        kxi_at, part_at, item_at, fault_at, dofs_at, star_at, send_at = 0, 1, 2, 3, 7, 8, 9
        proj_at, orient_at, near_at, code_at = range(10, 14)
        asked_at, slot_at, work_at, sends_at = 0, 1, 2, 3
        trace_table_at, turn_table_at, near_out, code_out = range(7, 11)
        kxi_ref = ins[kxi_at]
        table_ref[...] = table(jnp.concatenate([kxi_ref[d].T for d in range(DIMS)], axis=0))
        by_row = lax.broadcasted_iota(jnp.int32, (faults, faults), 0)
        by_lane = lax.broadcasted_iota(jnp.int32, (faults, faults), 1)
        across = ins[part_at][...]
        wide = jnp.broadcast_to(across, (faults, faults))
        down = jnp.sum(jnp.where(by_row == by_lane, wide, 0), axis=1, keepdims=True)
        rank = jnp.sum(
            jnp.where((down == across) & (by_row < by_lane), 1, 0), axis=0, keepdims=True
        )
        place = across * slot_most + rank
        outs[slot_at][...] = place
        outs.flush(slot_at)
        chosen = one_hot(0, slots, place)
        item = (ins[item_at][...] + 1).astype(f32)
        rows = [pad_rows(ins[fault_at + i][...], node_pad) for i in range(4)]
        rows.append(pad_rows(item, LANES - item_row))
        head, rest = split(jnp.concatenate(rows, axis=0))
        outs[asked_at][...] = lax.dot_general(
            jnp.concatenate([chosen, chosen], axis=1),
            jnp.concatenate([head, rest], axis=1).astype(half),
            (((1,), (1,)), ((), ())),
            preferred_element_type=f32,
        )
        outs.flush(asked_at)

        proj_ref, orient_ref = ins[proj_at], ins[orient_at]
        outs[trace_table_at][...] = table(
            jnp.concatenate([pad_rows(proj_ref[:, j, :], node_pad) for j in range(FACES)], axis=0)
        )
        outs[turn_table_at][...] = table(
            jnp.concatenate(
                [pad_lanes(pad_rows(orient_ref[t].T, node_pad), node_pad) for t in range(TURNS)],
                axis=0,
            )
        )
        odd_row, odd_col = odd_place()
        near = flat_row(ins[near_at])
        block = (near // ghosts) % 4
        flip = jnp.where(block < 2, jnp.where(odd_row, 0, 1), jnp.where(odd_col, 0, 1))
        outs[near_out][...] = jnp.where(
            near < sides_all, near, near + ghosts * flip * (1 - 2 * (block % 2))
        )
        outs[code_out][...] = flat_row(ins[code_at])

        dofs_ref, work_ref = ins[dofs_at], outs[work_at]
        for q in range(QUANT):
            start = dofs_ref[q * basis : (q + 1) * basis, :]
            work_ref[q * basis : (q + 1) * basis, :] = time_step * start
            piece_ref[q] = pieces(start)
        star_ref = ins[star_at]

        def advance(order_k, factor):
            for q in range(QUANT):
                moved_ref[q] = product(table_ref[...], piece_ref[q])
            factor = factor * time_step / (order_k + 1).astype(f32)
            for side in range(sides):
                lanes = slice(side * LANES, (side + 1) * LANES)

                def emit(p, value):
                    piece_ref[p, :, lanes] = pieces(value)
                    rows = slice(p * basis, (p + 1) * basis)
                    work_ref[rows, lanes] = work_ref[rows, lanes] + factor * value

                star_apply(star_ref, moved_ref, basis, side, emit)
            return factor

        lax.fori_loop(1, ORDER, advance, f32(time_step))
        outs.flush(work_at)
        picks = ins[send_at][...]
        picks = jnp.concatenate([picks, picks], axis=1)
        order = [
            jnp.where(odd_row, picks[1:2], picks[0:1]),
            jnp.where(odd_row, picks[0:1], picks[1:2]),
            jnp.where(odd_col, picks[3:4], picks[2:3]),
            jnp.where(odd_col, picks[2:3], picks[3:4]),
        ]
        width = 2 * ghosts
        chosen = jnp.concatenate([one_hot(0, elems, order[d]) for d in range(4)], axis=1)
        low = lax.broadcasted_iota(jnp.int32, (basis, width), 1) < ghosts
        got = []
        for q in range(QUANT):
            head, rest = split(work_ref[q * basis : (q + 1) * basis, :])
            both = product(jnp.concatenate([head, rest], axis=0).astype(half), chosen)
            got.append(both[:basis] + both[basis:])
        for d in range(4):
            lanes = slice(d * width, (d + 1) * width)
            for q in range(left_q):
                first = got[q][:, lanes]
                second = got[q + left_q][:, lanes] if q + left_q < QUANT else first
                outs[sends_at + d][q * basis : (q + 1) * basis, :] = jnp.where(low, first, second)

    def asked_item(asked):
        return asked[item_row : item_row + 1, :].astype(jnp.int32) - 1

    def local_kernel(ins, outs, left_ref, chosen_ref, wanted_ref):
        near_at, trace_table_at, work_at, code_at, asked_at = range(5)
        seen_at, fric_at, slot_seen_at, slot_near_at, slot_code_at = range(5)
        trace_table = ins[trace_table_at][...]
        work_ref = ins[work_at]
        kept = {}
        for q in range(QUANT):
            got = product(trace_table, pieces(work_ref[q * basis : (q + 1) * basis, :]))
            if q in first_q:
                kept[q] = got
            for j in range(FACES):
                head, rest = split(got[j * node_pad : (j + 1) * node_pad])
                left_ref[q * pair : (q + 1) * pair, j * elems : (j + 1) * elems] = jnp.concatenate(
                    [head, rest], axis=0
                ).astype(half)
        near = ins[near_at][...]
        for j in range(FACES):
            chosen_ref[j * elems : (j + 1) * elems, :] = one_hot(j * elems, elems, near)
        outs[seen_at][...] = product(left_ref[...], chosen_ref[...]).astype(half)
        item = asked_item(ins[asked_at][...].T)
        wanted_ref[...] = one_hot(0, sides_all, item)
        near_head, near_rest = split(near.astype(f32))
        shear, normal = [], []
        for j in range(FACES):
            rows = slice(j * node_pad, (j + 1) * node_pad)
            shear.append(0.5 * (kept[3][rows] + kept[6][rows]))
            normal.append(0.5 * kept[0][rows])
        rows = [*split(jnp.concatenate(shear, axis=1)), *split(jnp.concatenate(normal, axis=1))]
        rows += [near_head, near_rest, ins[code_at][...].astype(f32)]
        rows = jnp.concatenate(rows, axis=0)
        taken = product(pad_rows(rows, up(rows.shape[0], 16)).astype(half), wanted_ref[...])
        outs[fric_at][:node_pad, :] = taken[:node_pad] + taken[node_pad:pair]
        outs[fric_at][node_pad:, :] = taken[pair : pair + node_pad] + taken[pair + node_pad : 2 * pair]
        slot_near = (taken[2 * pair : 2 * pair + 1] + taken[2 * pair + 1 : 2 * pair + 2]).astype(jnp.int32)
        slot_near = jnp.where(item < 0, -1, slot_near)
        outs[slot_near_at][...] = slot_near
        outs[slot_code_at][...] = taken[2 * pair + 2 : 2 * pair + 3].astype(jnp.int32)
        left = jnp.concatenate([left_ref[q * pair : (q + 1) * pair, :] for q in first_q], axis=0)
        outs[slot_seen_at][...] = product(left, one_hot(0, sides_all, slot_near)).astype(half)

    def seen_across(
        got_refs, quants, trace_table, turn_table, near, code, seen_ref, chosen_ref, left_ref, emit
    ):
        low = lax.broadcasted_iota(jnp.int32, (basis, 2 * ghosts), 1) < ghosts
        for j in range(FACES):
            chosen_ref[j * ghost_all : (j + 1) * ghost_all, :] = one_hot(
                sides_all + j * ghost_all, ghost_all, near
            )
        for at, q in enumerate(quants):
            halves = []
            for first, second in (got_refs[:2], got_refs[2:]):
                if q < left_q:
                    rows = slice(q * basis, (q + 1) * basis)
                    a, b = first[rows, :], pltpu.roll(second[rows, :], ghosts, 1)
                else:
                    rows = slice((q - left_q) * basis, (q - left_q + 1) * basis)
                    a, b = pltpu.roll(first[rows, :], ghosts, 1), second[rows, :]
                halves.append(jnp.where(low, a, b))
            got = product(trace_table, pieces(jnp.concatenate(halves, axis=1)))
            for j in range(FACES):
                head, rest = split(got[j * node_pad : (j + 1) * node_pad])
                left_ref[
                    at * pair : (at + 1) * pair, j * ghost_all : (j + 1) * ghost_all
                ] = jnp.concatenate([head, rest], axis=0).astype(half)
        found = product(left_ref[...], chosen_ref[...])
        is_zero = jnp.broadcast_to(code, (node_pad, code.shape[1])) == 0
        is_one = jnp.broadcast_to(code, (node_pad, code.shape[1])) == 1
        for at, q in enumerate(quants):
            both = found[at * pair : (at + 1) * pair]
            both = both + seen_ref[at * pair : (at + 1) * pair].astype(f32)
            right = pad_rows(jnp.concatenate([both, both[:node_pad]], axis=0), turn_depth)
            rotated = product(turn_table, right.astype(half))
            emit(
                q,
                jnp.where(
                    is_zero,
                    rotated[:node_pad],
                    jnp.where(is_one, rotated[node_pad : 2 * node_pad], rotated[2 * node_pad :]),
                ),
            )

    def friction_kernel(ins, outs, chosen_ref, left_ref, wide_ref):
        got_at = range(4)
        trace_table_at, turn_table_at, near_at, code_at, seen_at, fric_at, asked_at = range(4, 11)
        back_at, slip_at = range(2)
        kept = {}

        def emit(q, value):
            kept[q] = value

        seen_across(
            [ins[i] for i in got_at],
            first_q,
            ins[trace_table_at][...],
            ins[turn_table_at][...],
            ins[near_at][...],
            ins[code_at][...],
            ins[seen_at],
            chosen_ref,
            left_ref,
            emit,
        )
        fric_ref = ins[fric_at]
        asked = ins[asked_at][...].T
        own = [asked[i * node_pad : (i + 1) * node_pad] for i in range(4)]
        slip = friction_solve(
            fric_ref[:node_pad, :] + 0.5 * (kept[3] - kept[6]),
            fric_ref[node_pad:, :] + 0.5 * kept[0],
            *own,
        )
        wide_ref[...] = pad_rows(slip, LANES).T
        packed = wide_ref[pl.ds(0, slots // per_row, stride=per_row), :]
        for k in range(1, per_row):
            part = wide_ref[pl.ds(k, slots // per_row, stride=per_row), :]
            packed = packed + pltpu.roll(part, k * slot_lanes, 1)
        outs[back_at][...] = packed
        outs[slip_at][...] = slip
        outs.flush(slip_at)

    def final_kernel(ins, outs, moved_ref, trace_ref, turned_ref, mixed_ref, chosen_ref, left_ref):
        got_at = range(4)
        trace_table_at, turn_table_at, near_at, code_at, seen_at, asked_at, slip_at = range(4, 11)
        work_at, lift_at, kxi_at, flux_at, star_at, dofs_at = range(11, 17)

        def emit(q, value):
            turned_ref[q * node_pad : (q + 1) * node_pad, :] = value

        seen_across(
            [ins[i] for i in got_at],
            range(QUANT),
            ins[trace_table_at][...],
            ins[turn_table_at][...],
            ins[near_at][...],
            ins[code_at][...],
            ins[seen_at],
            chosen_ref,
            left_ref,
            emit,
        )
        asked = ins[asked_at][...].T
        wanted = one_hot(0, sides_all, asked_item(asked))
        slip_head, slip_rest = split(ins[slip_at][...])
        pushed = lax.dot_general(
            jnp.concatenate([slip_head, slip_rest], axis=0).astype(half),
            wanted,
            (((1,), (1,)), ((), ())),
            preferred_element_type=f32,
        )
        pushed = 2.0 * (pushed[:node_pad] + pushed[node_pad:])
        kxi_ref, lift_ref, work_ref = ins[kxi_at], ins[lift_at], ins[work_at]
        back_table = table(jnp.concatenate([kxi_ref[d] for d in range(DIMS)], axis=0))
        lift_table = jnp.concatenate(
            [table(pad_lanes(lift_ref[:, j, :].T, node_pad)) for j in range(FACES)], axis=1
        )
        trace_table = ins[trace_table_at][...]
        for q in range(QUANT):
            right = pieces(work_ref[q * basis : (q + 1) * basis, :])
            moved_ref[q] = product(back_table, right)
            trace_ref[q] = product(trace_table, right)
        flux_ref = ins[flux_at]
        for side in range(sides):
            lanes = slice(side * LANES, (side + 1) * LANES)
            for j in range(FACES):
                at = j * elems + side * LANES
                totals = flux_apply(
                    flux_ref,
                    0,
                    lambda q: trace_ref[q, j * node_pad : (j + 1) * node_pad, lanes],
                    j,
                    side,
                    [None] * QUANT,
                )
                totals = flux_apply(
                    flux_ref,
                    1,
                    lambda q: turned_ref[q * node_pad : (q + 1) * node_pad, at : at + LANES],
                    j,
                    side,
                    totals,
                )
                push = pushed[:, at : at + LANES]
                totals[3] = totals[3] - push
                totals[6] = totals[6] + push
                for p in range(QUANT):
                    mixed_ref[p, j * turn_depth : (j + 1) * turn_depth, lanes] = pieces(totals[p])
        star_ref, dofs_ref = ins[star_at], ins[dofs_at]
        out_ref = outs[0]
        for side in range(sides):
            lanes = slice(side * LANES, (side + 1) * LANES)

            def emit(p, value):
                rows = slice(p * basis, (p + 1) * basis)
                out_ref[rows, lanes] = dofs_ref[rows, lanes] + 0.25 * value

            star_apply(star_ref, moved_ref, basis, side, emit)
        for p in range(QUANT):
            rows = slice(p * basis, (p + 1) * basis)
            out_ref[rows, :] = out_ref[rows, :] + 0.25 * product(lift_table, mixed_ref[p])

    def return_kernel(ins, outs):
        place = ins[0][...]
        held = ins[1][...].T
        rows = slots // per_row
        got = jnp.zeros((pair, faults), f32)
        for k in range(per_row):
            head, rest = split(held[k * slot_lanes : k * slot_lanes + node_pad])
            chosen = one_hot(0, rows, jnp.where(place % per_row == k, place // per_row, -1))
            got = got + product(jnp.concatenate([head, rest], axis=0).astype(half), chosen)
        outs[0][...] = (got[:node_pad] + got[node_pad:])[:nodes]

    vmem = pltpu.VMEM
    proj_rows = jnp.transpose(face_proj, (2, 0, 1))
    lift_rows = jnp.transpose(face_lift, (1, 0, 2))
    *first_outs, trace_table, turn_table, near, code = call(
        predict_kernel,
        "predict",
        [
            kxi,
            fault_part.reshape(1, faults),
            fault_item.reshape(1, faults),
            shear_init,
            normal_init,
            state_var,
            slip_prev,
            dofs,
            star,
            send_list,
            proj_rows,
            orient,
            neighbour,
            orient_code,
        ],
        [
            ((slots, LANES), f32, "hbm"),
            ((1, faults), jnp.int32, "vmem"),
            (dofs.shape, f32, "vmem"),
        ]
        + [((left_q * basis, 2 * ghosts), f32, "any")] * 4
        + [
            ((FACES * node_pad, depth), half, "vmem"),
            ((TURNS * node_pad, turn_depth), half, "vmem"),
            ((1, sides_all), jnp.int32, "vmem"),
            ((1, sides_all), jnp.int32, "vmem"),
        ],
        scratch=(
            vmem((QUANT, DIMS * basis, elems), f32),
            vmem((QUANT, depth, elems), half),
            vmem((DIMS * basis, depth), half),
        ),
        flops=5 * 2 * DIMS * basis * depth * QUANT * elems,
        moved=8_000_000,
    )

    asked, slot_of, work, *sends = first_outs
    asked = lax.all_to_all(
        asked.reshape(devices, slot_most, LANES), ("row", "col"), split_axis=0, concat_axis=0, tiled=True
    ).reshape(slots, LANES)

    def swapped(values, axis, first):
        pairs = [(i, i + 1) for i in range(first, lax.axis_size(axis) - 1, 2)]
        return lax.ppermute(values, axis, pairs + [(b, a) for a, b in pairs])

    arrived = [
        swapped(sends[0], "row", 0),
        swapped(sends[1], "row", 1),
        swapped(sends[2], "col", 0),
        swapped(sends[3], "col", 1),
    ]

    seen, fric, slot_seen, slot_near, slot_code = call(
        local_kernel,
        "local_terms",
        [Kept(one) for one in (near, trace_table, work, code, asked)],
        [
            ((QUANT * pair, sides_all), half, "vmem"),
            ((pair, slots), f32, "vmem"),
            ((len(first_q) * pair, slots), half, "vmem"),
            ((1, slots), jnp.int32, "vmem"),
            ((1, slots), jnp.int32, "vmem"),
        ],
        scratch=(
            vmem((QUANT * pair, sides_all), half),
            vmem((sides_all, sides_all), half),
            vmem((sides_all, slots), half),
        ),
        flops=2 * QUANT * pair * sides_all * sides_all,
        moved=8_000_000,
    )

    back, slip = call(
        friction_kernel,
        "friction",
        [
            Kept(one)
            for one in (*arrived, trace_table, turn_table, slot_near, slot_code, slot_seen, fric, asked)
        ],
        [((slots // per_row, LANES), f32, "any"), ((node_pad, slots), f32, "vmem")],
        scratch=(
            vmem((FACES * ghost_all, slots), half),
            vmem((len(first_q) * pair, FACES * ghost_all), half),
            vmem((slots, LANES), f32),
        ),
        flops=2 * len(first_q) * pair * sides_all * slots,
        moved=4_000_000,
    )
    back = lax.all_to_all(
        back.reshape(devices, *chunk_shape), ("row", "col"), split_axis=0, concat_axis=0, tiled=True
    ).reshape(slots // per_row, LANES)

    (dofs_next,) = call(
        final_kernel,
        "final_terms",
        [
            *(Kept(one) for one in arrived),
            Kept(trace_table),
            Kept(turn_table),
            Kept(near),
            Kept(code),
            Kept(seen),
            Kept(asked),
            Kept(slip),
            Kept(work),
            lift_rows,
            kxi,
            flux_mats,
            star,
            dofs,
        ],
        [(dofs.shape, f32, "any")],
        scratch=(
            vmem((QUANT, DIMS * basis, elems), f32),
            vmem((QUANT, FACES * node_pad, elems), f32),
            vmem((QUANT * node_pad, sides_all), f32),
            vmem((QUANT, FACES * turn_depth, elems), half),
            vmem((FACES * ghost_all, sides_all), half),
            vmem((QUANT * pair, FACES * ghost_all), half),
        ),
        flops=2 * QUANT * pair * sides_all * sides_all,
        moved=8_000_000,
    )

    (slip_rate,) = call(
        return_kernel,
        "fault_return",
        [Kept(slot_of), Kept(back)],
        [((nodes, faults), f32, "any")],
        flops=2 * pair * slots * faults,
        moved=200_000,
    )
    return dofs_next, slip_rate


def solution(mesh):
    across = ("row", "col")
    placed = (
        P(None, across),
        P(None, across),
        P(None, across),
        P(),
        P(),
        P(),
        P(),
        P(None, across),
        P(None, across),
        P(None, across),
        P(across, None),
        P(across),
        P(None, across),
        P(None, across),
        P(None, across),
        P(None, across),
    )
    return jax.shard_map(
        per_device,
        mesh=mesh,
        in_specs=placed,
        out_specs=(P(None, across), P(None, across)),
        check_vma=False,
    )
```

```python
import jax
import jax.numpy as jnp
from jax import lax
from jax.experimental import pallas as pl
from jax.experimental.pallas import tpu as pltpu
from jax.sharding import PartitionSpec as P

QUANT = 9
ORDER = 6
NEWTON_ITERS = 3
FACES = 4
DIMS = 3
TURNS = 3

time_step = 2.0
fric_a = 0.5
f32 = jnp.float32
half = jnp.bfloat16
MIB = 2**20
LANES = 128
SUB = 8


def up(count, unit):
    return -(-count // unit) * unit


def friction_solve(shear, normal, shear_init, normal_init, state_var, slip_prev):
    shear_total = shear_init + shear
    strength = fric_a * (normal_init * (1.0 + 0.5 * jnp.tanh(normal)))
    growth = jnp.exp(state_var / fric_a) * 0.5
    steep = strength * growth
    slip_now = slip_prev
    for newton_step in range(NEWTON_ITERS):
        scaled = growth * slip_now
        root = jnp.sqrt(1.0 + scaled * scaled)
        positive = jnp.log(jnp.abs(scaled) + root)
        misfit = shear_total - slip_now - strength * jnp.where(scaled < 0.0, -positive, positive)
        slip_now = slip_now + misfit / (1.0 + steep / root)
    return slip_now


def split(values):
    head = values.astype(half).astype(f32)
    return head, values - head


def pad_rows(values, rows):
    if values.shape[0] == rows:
        return values
    return jnp.concatenate(
        [values, jnp.zeros((rows - values.shape[0], values.shape[1]), f32)], axis=0
    )


def pad_lanes(values, lanes):
    if values.shape[1] == lanes:
        return values
    return jnp.concatenate(
        [values, jnp.zeros((values.shape[0], lanes - values.shape[1]), f32)], axis=1
    )


def pieces(values):
    head, rest = split(values)
    return pad_rows(jnp.concatenate([head, rest, head], axis=0), up(3 * values.shape[0], 16)).astype(
        half
    )


def table(values):
    head, rest = split(values)
    return pad_lanes(
        jnp.concatenate([head, head, rest], axis=1), up(3 * values.shape[1], 16)
    ).astype(half)


def product(left, right):
    return jnp.dot(left, right, preferred_element_type=f32)


def lane_row(ref, row, side):
    return ref[row : row + 1, side * LANES : (side + 1) * LANES]


def one_hot(first, rows, index_row):
    places = lax.broadcasted_iota(jnp.int32, (rows, index_row.shape[1]), 0) + first
    return jnp.where(places == index_row, 1.0, 0.0).astype(half)


def flat_row(ref):
    return jnp.concatenate([ref[i : i + 1, :] for i in range(ref.shape[0])], axis=1)


def star_group(star_ref, part_of, side, first, count):
    totals = [None] * count
    for inner in range(QUANT):
        for axis_dir in range(DIMS):
            part = part_of(inner, axis_dir)
            for i in range(count):
                at = (axis_dir * QUANT + first + i) * QUANT + inner
                term = lane_row(star_ref, at, side) * part
                totals[i] = term if totals[i] is None else totals[i] + term
    return totals


def star_apply(star_ref, part_of, side, emit, group=3):
    for first in range(0, QUANT, group):
        for i, total in enumerate(star_group(star_ref, part_of, side, first, group)):
            emit(first + i, total)


def flux_apply(flux_ref, which, values_of, face, side, totals):
    for inner in range(QUANT):
        value = values_of(inner)
        for p in range(QUANT):
            at = ((face * 2 + which) * QUANT + p) * QUANT + inner
            term = lane_row(flux_ref, at, side) * value
            totals[p] = term if totals[p] is None else totals[p] + term
    return totals


class Kept:
    def __init__(self, array):
        self.array = array


class Inputs:
    def __init__(self, sources, targets, sems):
        self.sources, self.targets, self.waiting = sources, targets, {}
        for i, (source, target) in enumerate(zip(sources, targets)):
            if source is target:
                continue
            self.waiting[i] = pltpu.make_async_copy(source, target, sems.at[i])
            self.waiting[i].start()

    def __getitem__(self, i):
        if i in self.waiting:
            self.waiting.pop(i).wait()
        return self.targets[i]

    def rest(self):
        for move in self.waiting.values():
            move.wait()


class Outputs:
    def __init__(self, targets, sources, sems):
        self.targets, self.sources, self.sems = targets, sources, sems
        self.moving = []

    def __getitem__(self, i):
        return self.targets[i] if self.sources[i] is None else self.sources[i]

    def flush(self, i, rows=None):
        source, target = self.sources[i], self.targets[i]
        if source is None:
            return
        if rows is not None:
            source, target = source.at[rows], target.at[rows]
        move = pltpu.make_async_copy(source, target, self.sems.at[len(self.moving)])
        move.start()
        self.moving.append(move)

    def wait(self):
        for move in self.moving:
            move.wait()


def call(kernel, name, ins, outs, scratch=(), flops=0, moved=0, room=32, flushes=None):
    n_in, n_out = len(ins), len(outs)
    placed = [i for i, one in enumerate(outs) if one[2] == "hbm"]
    stays = [isinstance(one, Kept) for one in ins]
    brought = [i for i in range(n_in) if not isinstance(ins[i], Kept)]
    ins = [one.array if isinstance(one, Kept) else one for one in ins]
    flushes = flushes or max(1, len(placed))

    def body(*refs):
        sources, targets = refs[:n_in], refs[n_in : n_in + n_out]
        at = n_in + n_out
        held = list(sources)
        for i in brought:
            held[i], at = refs[at], at + 1
        kept, at = refs[at : at + len(placed)], at + len(placed)
        in_sems, out_sems, *more = refs[at:]
        source_of = [None] * n_out
        for i, ref in zip(placed, kept):
            source_of[i] = ref
        inputs = Inputs(sources, held, in_sems)
        outputs = Outputs(targets, source_of, out_sems)
        kernel(inputs, outputs, *more)
        inputs.rest()
        outputs.wait()

    shapes = [
        {"hbm": pltpu.HBM, "vmem": pltpu.VMEM, "any": jax.ShapeDtypeStruct}[one[2]](one[0], one[1])
        for one in outs
    ]
    spaces = [pltpu.VMEM if one else pltpu.HBM for one in stays]
    return pl.pallas_call(
        body,
        name=name,
        out_shape=shapes,
        in_specs=[pl.BlockSpec(memory_space=space) for space in spaces],
        scratch_shapes=[
            *(pltpu.VMEM(ins[i].shape, ins[i].dtype) for i in brought),
            *(pltpu.VMEM(outs[i][0], outs[i][1]) for i in placed),
            pltpu.SemaphoreType.DMA((max(1, n_in),)),
            pltpu.SemaphoreType.DMA((flushes,)),
            *scratch,
        ],
        cost_estimate=pl.CostEstimate(flops=flops, bytes_accessed=moved, transcendentals=0),
        compiler_params=pltpu.CompilerParams(vmem_limit_bytes=room * MIB),
    )(*(pltpu.with_memory_space_constraint(a, space) for a, space in zip(ins, spaces)))


def per_device(
    dofs,
    star,
    flux_mats,
    kxi,
    face_proj,
    face_lift,
    orient,
    neighbour,
    orient_code,
    send_list,
    fault_part,
    fault_item,
    shear_init,
    normal_init,
    state_var,
    slip_prev,
):
    basis = kxi.shape[1]
    nodes = face_proj.shape[2]
    elems = dofs.shape[1]
    sides = elems // LANES
    ghosts = send_list.shape[1]
    ghost_all = 4 * ghosts
    node_pad = up(nodes, SUB)
    faults = fault_item.shape[0]
    devices = lax.axis_size("row") * lax.axis_size("col")
    slot_most = max(2, 2 * faults // devices)
    slots = devices * slot_most
    sides_all = FACES * elems
    left_q = QUANT // 2
    cut = up(basis // 2, SUB)
    halo_rows = left_q * basis + cut
    depth = up(3 * basis, 16)
    turn_depth = up(3 * node_pad, 16)
    item_row = 4 * node_pad
    pair = 2 * node_pad
    first_q = (0, 3, 6)
    slot_lanes = up(node_pad, 32)
    per_row = LANES // slot_lanes
    chunk = slot_most * slot_lanes
    chunk_shape = (chunk // LANES, LANES) if chunk % LANES == 0 else (chunk,)

    def odd_place():
        return lax.axis_index("row") % 2 == 1, lax.axis_index("col") % 2 == 1

    def predict_kernel(ins, outs, table_ref, chosen_ref, *by_side):
        moved_refs, piece_refs = by_side[:sides], by_side[sides:]
        kxi_at, dofs_at, star_at, part_at, item_at, fault_at, send_at = 0, 1, 2, 3, 4, 5, 9
        proj_at, orient_at, near_at, code_at = range(10, 14)
        asked_at, slot_at, work_at, sends_at = 0, 1, 2, 3
        trace_table_at, turn_table_at, near_out, code_out = range(7, 11)
        lanes_of = [slice(side * LANES, (side + 1) * LANES) for side in range(sides)]
        kxi_ref = ins[kxi_at]
        table_ref[...] = table(jnp.concatenate([kxi_ref[d].T for d in range(DIMS)], axis=0))
        dofs_ref, work_ref = ins[dofs_at], outs[work_at]
        for q in range(QUANT):
            rows = slice(q * basis, (q + 1) * basis)
            for side in range(sides):
                start = dofs_ref[rows, lanes_of[side]]
                work_ref[rows, lanes_of[side]] = time_step * start
                piece_refs[side][q] = pieces(start)

        def multiply(side):
            for q in range(0, QUANT, 2):
                quants = range(q, min(q + 2, QUANT))
                right = jnp.concatenate([piece_refs[side][one] for one in quants], axis=1)
                got = product(table_ref[...], right)
                for i, one in enumerate(quants):
                    moved_refs[side][one] = got[:, i * LANES : (i + 1) * LANES]

        def part_of(side):
            return lambda q, d: moved_refs[side][q, d * basis : (d + 1) * basis, :]

        multiply(0)
        by_row = lax.broadcasted_iota(jnp.int32, (faults, faults), 0)
        by_lane = lax.broadcasted_iota(jnp.int32, (faults, faults), 1)
        across = ins[part_at][...]
        wide = jnp.broadcast_to(across, (faults, faults))
        down = jnp.sum(jnp.where(by_row == by_lane, wide, 0), axis=1, keepdims=True)
        rank = jnp.sum(
            jnp.where((down == across) & (by_row < by_lane), 1, 0), axis=0, keepdims=True
        )
        place = across * slot_most + rank
        outs[slot_at][...] = place
        chosen = one_hot(0, slots, place)
        item = (ins[item_at][...] + 1).astype(f32)
        rows = [pad_rows(ins[fault_at + i][...], node_pad) for i in range(4)]
        rows.append(pad_rows(item, LANES - item_row))
        head, rest = split(jnp.concatenate(rows, axis=0))
        outs[asked_at][...] = lax.dot_general(
            jnp.concatenate([chosen, chosen], axis=1),
            jnp.concatenate([head, rest], axis=1).astype(half),
            (((1,), (1,)), ((), ())),
            preferred_element_type=f32,
        )
        outs.flush(asked_at)
        proj_ref, orient_ref = ins[proj_at], ins[orient_at]
        outs[trace_table_at][...] = table(
            jnp.concatenate([pad_rows(proj_ref[:, j, :], node_pad) for j in range(FACES)], axis=0)
        )
        outs[turn_table_at][...] = table(
            jnp.concatenate(
                [pad_lanes(pad_rows(orient_ref[t].T, node_pad), node_pad) for t in range(TURNS)],
                axis=0,
            )
        )
        odd_row, odd_col = odd_place()
        near = flat_row(ins[near_at])
        block = (near // ghosts) % 4
        flip = jnp.where(block < 2, jnp.where(odd_row, 0, 1), jnp.where(odd_col, 0, 1))
        outs[near_out][...] = jnp.where(
            near < sides_all, near, near + ghosts * flip * (1 - 2 * (block % 2))
        )
        outs[code_out][...] = flat_row(ins[code_at])
        picks = ins[send_at][...]
        picks = jnp.concatenate([picks, picks], axis=1)
        order = [
            jnp.where(odd_row, picks[1:2], picks[0:1]),
            jnp.where(odd_row, picks[0:1], picks[1:2]),
            jnp.where(odd_col, picks[3:4], picks[2:3]),
            jnp.where(odd_col, picks[2:3], picks[3:4]),
        ]
        width = 2 * ghosts
        for d in range(4):
            chosen_ref[:, d * width : (d + 1) * width] = one_hot(0, elems, order[d])
        star_ref = ins[star_at]

        def advance(order_k, factor):
            factor = factor * time_step / (order_k + 1).astype(f32)
            for side in range(sides):
                lanes = lanes_of[side]

                def emit(p, value):
                    piece_refs[side][p] = pieces(value)
                    rows = slice(p * basis, (p + 1) * basis)
                    work_ref[rows, lanes] = work_ref[rows, lanes] + factor * value

                multiply((side + 1) % sides)
                star_apply(star_ref, part_of(side), side, emit)
            return factor

        factor = lax.fori_loop(1, ORDER - 1, advance, f32(time_step))
        factor = factor * (time_step / ORDER)

        for side in range(sides):
            lanes = lanes_of[side]

            def emit_last(p, value):
                rows = slice(p * basis, (p + 1) * basis)
                work_ref[rows, lanes] = work_ref[rows, lanes] + factor * value

            if side + 1 < sides:
                multiply(side + 1)
            star_apply(star_ref, part_of(side), side, emit_last)
        heads, rests = split(work_ref[...])
        both = product(jnp.concatenate([heads, rests], axis=0).astype(half), chosen_ref[...])
        got = both[: QUANT * basis] + both[QUANT * basis :]
        right = pad_rows(got[halo_rows:], halo_rows)
        low = lax.broadcasted_iota(jnp.int32, (halo_rows, width), 1) < ghosts
        for d in range(4):
            lanes = slice(d * width, (d + 1) * width)
            outs[sends_at + d][...] = jnp.where(low, got[:halo_rows, lanes], right[:, lanes])

    def asked_item(asked):
        return asked[item_row : item_row + 1, :].astype(jnp.int32) - 1

    def local_kernel(ins, outs, left_ref, chosen_ref, wanted_ref):
        near_at, trace_table_at, work_at, code_at, asked_at = range(5)
        seen_at, fric_at, slot_seen_at, slot_near_at, slot_code_at = range(5)
        trace_table = ins[trace_table_at][...]
        work_ref = ins[work_at]
        kept = {}
        for q in range(QUANT):
            got = product(trace_table, pieces(work_ref[q * basis : (q + 1) * basis, :]))
            if q in first_q:
                kept[q] = got
            for j in range(FACES):
                head, rest = split(got[j * node_pad : (j + 1) * node_pad])
                left_ref[q * pair : (q + 1) * pair, j * elems : (j + 1) * elems] = jnp.concatenate(
                    [head, rest], axis=0
                ).astype(half)
        near = ins[near_at][...]
        for j in range(FACES):
            chosen_ref[j * elems : (j + 1) * elems, :] = one_hot(j * elems, elems, near)
        outs[seen_at][...] = product(left_ref[...], chosen_ref[...]).astype(half)
        item = asked_item(ins[asked_at][...].T)
        wanted_ref[...] = one_hot(0, sides_all, item)
        near_head, near_rest = split(near.astype(f32))
        shear, normal = [], []
        for j in range(FACES):
            rows = slice(j * node_pad, (j + 1) * node_pad)
            shear.append(0.5 * (kept[3][rows] + kept[6][rows]))
            normal.append(0.5 * kept[0][rows])
        rows = [*split(jnp.concatenate(shear, axis=1)), *split(jnp.concatenate(normal, axis=1))]
        rows += [near_head, near_rest, ins[code_at][...].astype(f32)]
        rows = jnp.concatenate(rows, axis=0)
        taken = product(pad_rows(rows, up(rows.shape[0], 16)).astype(half), wanted_ref[...])
        outs[fric_at][:node_pad, :] = taken[:node_pad] + taken[node_pad:pair]
        outs[fric_at][node_pad:, :] = taken[pair : pair + node_pad] + taken[pair + node_pad : 2 * pair]
        slot_near = (taken[2 * pair : 2 * pair + 1] + taken[2 * pair + 1 : 2 * pair + 2]).astype(jnp.int32)
        slot_near = jnp.where(item < 0, -1, slot_near)
        outs[slot_near_at][...] = slot_near
        outs[slot_code_at][...] = taken[2 * pair + 2 : 2 * pair + 3].astype(jnp.int32)
        left = jnp.concatenate([left_ref[q * pair : (q + 1) * pair, :] for q in first_q], axis=0)
        outs[slot_seen_at][...] = product(left, one_hot(0, sides_all, slot_near)).astype(half)

    def seen_across(
        got_refs, quants, trace_table, turn_table, near, code, seen_ref, chosen_ref, left_ref, emit
    ):
        def joined(first, second, begin, end):
            low = lax.broadcasted_iota(jnp.int32, (end - begin, 2 * ghosts), 1) < ghosts
            if end <= halo_rows:
                rows = slice(begin, end)
                return jnp.where(low, first[rows, :], pltpu.roll(second[rows, :], ghosts, 1))
            rows = slice(begin - halo_rows, end - halo_rows)
            return jnp.where(low, pltpu.roll(first[rows, :], ghosts, 1), second[rows, :])

        def ghost_rows(first, second, begin, end):
            if begin < halo_rows < end:
                parts = [joined(first, second, begin, halo_rows), joined(first, second, halo_rows, end)]
                return jnp.concatenate(parts, axis=0)
            return joined(first, second, begin, end)

        for j in range(FACES):
            chosen_ref[j * ghost_all : (j + 1) * ghost_all, :] = one_hot(
                sides_all + j * ghost_all, ghost_all, near
            )
        for at, q in enumerate(quants):
            halves = [
                ghost_rows(first, second, q * basis, (q + 1) * basis)
                for first, second in (got_refs[:2], got_refs[2:])
            ]
            got = product(trace_table, pieces(jnp.concatenate(halves, axis=1)))
            for j in range(FACES):
                head, rest = split(got[j * node_pad : (j + 1) * node_pad])
                left_ref[
                    at * pair : (at + 1) * pair, j * ghost_all : (j + 1) * ghost_all
                ] = jnp.concatenate([head, rest], axis=0).astype(half)
        found = product(left_ref[...], chosen_ref[...])
        is_zero = jnp.broadcast_to(code, (node_pad, code.shape[1])) == 0
        is_one = jnp.broadcast_to(code, (node_pad, code.shape[1])) == 1
        for at, q in enumerate(quants):
            both = found[at * pair : (at + 1) * pair]
            both = both + seen_ref[at * pair : (at + 1) * pair].astype(f32)
            right = pad_rows(jnp.concatenate([both, both[:node_pad]], axis=0), turn_depth)
            rotated = product(turn_table, right.astype(half))
            emit(
                q,
                jnp.where(
                    is_zero,
                    rotated[:node_pad],
                    jnp.where(is_one, rotated[node_pad : 2 * node_pad], rotated[2 * node_pad :]),
                ),
            )

    def friction_kernel(ins, outs, chosen_ref, left_ref, wide_ref):
        got_at = range(4)
        trace_table_at, turn_table_at, near_at, code_at, seen_at, fric_at, asked_at = range(4, 11)
        back_at, slip_at = range(2)
        kept = {}

        def emit(q, value):
            kept[q] = value

        seen_across(
            [ins[i] for i in got_at],
            first_q,
            ins[trace_table_at][...],
            ins[turn_table_at][...],
            ins[near_at][...],
            ins[code_at][...],
            ins[seen_at],
            chosen_ref,
            left_ref,
            emit,
        )
        fric_ref = ins[fric_at]
        asked = ins[asked_at][...].T
        own = [asked[i * node_pad : (i + 1) * node_pad] for i in range(4)]
        slip = friction_solve(
            fric_ref[:node_pad, :] + 0.5 * (kept[3] - kept[6]),
            fric_ref[node_pad:, :] + 0.5 * kept[0],
            *own,
        )
        wide_ref[...] = pad_rows(slip, LANES).T
        packed = wide_ref[pl.ds(0, slots // per_row, stride=per_row), :]
        for k in range(1, per_row):
            part = wide_ref[pl.ds(k, slots // per_row, stride=per_row), :]
            packed = packed + pltpu.roll(part, k * slot_lanes, 1)
        outs[back_at][...] = packed
        outs[slip_at][...] = slip
        outs.flush(slip_at)

    def final_kernel(ins, outs, moved_ref, trace_ref, turned_ref, mixed_ref, chosen_ref, left_ref):
        got_at = range(4)
        trace_table_at, turn_table_at, near_at, code_at, seen_at, asked_at, slip_at = range(4, 11)
        work_at, lift_at, kxi_at, flux_at, star_at, dofs_at = range(11, 17)

        def emit(q, value):
            turned_ref[q * node_pad : (q + 1) * node_pad, :] = value

        seen_across(
            [ins[i] for i in got_at],
            range(QUANT),
            ins[trace_table_at][...],
            ins[turn_table_at][...],
            ins[near_at][...],
            ins[code_at][...],
            ins[seen_at],
            chosen_ref,
            left_ref,
            emit,
        )
        asked = ins[asked_at][...].T
        wanted = one_hot(0, sides_all, asked_item(asked))
        slip_head, slip_rest = split(ins[slip_at][...])
        pushed = lax.dot_general(
            jnp.concatenate([slip_head, slip_rest], axis=0).astype(half),
            wanted,
            (((1,), (1,)), ((), ())),
            preferred_element_type=f32,
        )
        pushed = 2.0 * (pushed[:node_pad] + pushed[node_pad:])
        kxi_ref, lift_ref, work_ref = ins[kxi_at], ins[lift_at], ins[work_at]
        back_table = table(jnp.concatenate([kxi_ref[d] for d in range(DIMS)], axis=0))
        lift_table = jnp.concatenate(
            [table(pad_lanes(lift_ref[:, j, :].T, node_pad)) for j in range(FACES)], axis=1
        )
        trace_table = ins[trace_table_at][...]
        for q in range(QUANT):
            right = pieces(work_ref[q * basis : (q + 1) * basis, :])
            moved_ref[q] = product(back_table, right)
            trace_ref[q] = product(trace_table, right)
        flux_ref = ins[flux_at]
        for side in range(sides):
            lanes = slice(side * LANES, (side + 1) * LANES)
            for j in range(FACES):
                at = j * elems + side * LANES
                totals = flux_apply(
                    flux_ref,
                    0,
                    lambda q: trace_ref[q, j * node_pad : (j + 1) * node_pad, lanes],
                    j,
                    side,
                    [None] * QUANT,
                )
                totals = flux_apply(
                    flux_ref,
                    1,
                    lambda q: turned_ref[q * node_pad : (q + 1) * node_pad, at : at + LANES],
                    j,
                    side,
                    totals,
                )
                push = pushed[:, at : at + LANES]
                totals[3] = totals[3] - push
                totals[6] = totals[6] + push
                for p in range(QUANT):
                    mixed_ref[p, j * turn_depth : (j + 1) * turn_depth, lanes] = pieces(totals[p])
        star_ref, dofs_ref = ins[star_at], ins[dofs_at]
        out_ref = outs[0]
        for side in range(sides):
            lanes = slice(side * LANES, (side + 1) * LANES)

            def emit(p, value):
                rows = slice(p * basis, (p + 1) * basis)
                out_ref[rows, lanes] = dofs_ref[rows, lanes] + 0.25 * value

            star_apply(
                star_ref,
                lambda q, d: moved_ref[q, d * basis : (d + 1) * basis, lanes],
                side,
                emit,
            )
        for p in range(QUANT):
            rows = slice(p * basis, (p + 1) * basis)
            out_ref[rows, :] = out_ref[rows, :] + 0.25 * product(lift_table, mixed_ref[p])

    def return_kernel(ins, outs):
        place = ins[0][...]
        held = ins[1][...].T
        rows = slots // per_row
        got = jnp.zeros((pair, faults), f32)
        for k in range(per_row):
            head, rest = split(held[k * slot_lanes : k * slot_lanes + node_pad])
            chosen = one_hot(0, rows, jnp.where(place % per_row == k, place // per_row, -1))
            got = got + product(jnp.concatenate([head, rest], axis=0).astype(half), chosen)
        outs[0][...] = (got[:node_pad] + got[node_pad:])[:nodes]

    vmem = pltpu.VMEM
    proj_rows = jnp.transpose(face_proj, (2, 0, 1))
    lift_rows = jnp.transpose(face_lift, (1, 0, 2))
    *first_outs, trace_table, turn_table, near, code = call(
        predict_kernel,
        "predict",
        [
            kxi,
            dofs,
            star,
            fault_part.reshape(1, faults),
            fault_item.reshape(1, faults),
            shear_init,
            normal_init,
            state_var,
            slip_prev,
            send_list,
            proj_rows,
            orient,
            neighbour,
            orient_code,
        ],
        [
            ((slots, LANES), f32, "hbm"),
            ((1, faults), jnp.int32, "vmem"),
            (dofs.shape, f32, "vmem"),
        ]
        + [((halo_rows, 2 * ghosts), f32, "any")] * 4
        + [
            ((FACES * node_pad, depth), half, "vmem"),
            ((TURNS * node_pad, turn_depth), half, "vmem"),
            ((1, sides_all), jnp.int32, "vmem"),
            ((1, sides_all), jnp.int32, "vmem"),
        ],
        scratch=(
            vmem((DIMS * basis, depth), half),
            vmem((elems, 8 * ghosts), half),
            *[vmem((QUANT, DIMS * basis, LANES), f32)] * sides,
            *[vmem((QUANT, depth, LANES), half)] * sides,
        ),
        flops=5 * 2 * DIMS * basis * depth * QUANT * elems,
        moved=8_000_000,
    )

    asked, slot_of, work, *sends = first_outs
    asked = lax.all_to_all(
        asked.reshape(devices, slot_most, LANES), ("row", "col"), split_axis=0, concat_axis=0, tiled=True
    ).reshape(slots, LANES)

    def swapped(values, axis, first):
        pairs = [(i, i + 1) for i in range(first, lax.axis_size(axis) - 1, 2)]
        return lax.ppermute(values, axis, pairs + [(b, a) for a, b in pairs])

    arrived = [
        swapped(sends[0], "row", 0),
        swapped(sends[1], "row", 1),
        swapped(sends[2], "col", 0),
        swapped(sends[3], "col", 1),
    ]

    seen, fric, slot_seen, slot_near, slot_code = call(
        local_kernel,
        "local_terms",
        [Kept(one) for one in (near, trace_table, work, code, asked)],
        [
            ((QUANT * pair, sides_all), half, "vmem"),
            ((pair, slots), f32, "vmem"),
            ((len(first_q) * pair, slots), half, "vmem"),
            ((1, slots), jnp.int32, "vmem"),
            ((1, slots), jnp.int32, "vmem"),
        ],
        scratch=(
            vmem((QUANT * pair, sides_all), half),
            vmem((sides_all, sides_all), half),
            vmem((sides_all, slots), half),
        ),
        flops=2 * QUANT * pair * sides_all * sides_all,
        moved=8_000_000,
    )

    back, slip = call(
        friction_kernel,
        "friction",
        [
            Kept(one)
            for one in (*arrived, trace_table, turn_table, slot_near, slot_code, slot_seen, fric, asked)
        ],
        [((slots // per_row, LANES), f32, "any"), ((node_pad, slots), f32, "vmem")],
        scratch=(
            vmem((FACES * ghost_all, slots), half),
            vmem((len(first_q) * pair, FACES * ghost_all), half),
            vmem((slots, LANES), f32),
        ),
        flops=2 * len(first_q) * pair * sides_all * slots,
        moved=4_000_000,
    )
    back = lax.all_to_all(
        back.reshape(devices, *chunk_shape), ("row", "col"), split_axis=0, concat_axis=0, tiled=True
    ).reshape(slots // per_row, LANES)

    (dofs_next,) = call(
        final_kernel,
        "final_terms",
        [
            *(Kept(one) for one in arrived),
            Kept(trace_table),
            Kept(turn_table),
            Kept(near),
            Kept(code),
            Kept(seen),
            Kept(asked),
            Kept(slip),
            Kept(work),
            lift_rows,
            kxi,
            flux_mats,
            star,
            dofs,
        ],
        [(dofs.shape, f32, "any")],
        scratch=(
            vmem((QUANT, DIMS * basis, elems), f32),
            vmem((QUANT, FACES * node_pad, elems), f32),
            vmem((QUANT * node_pad, sides_all), f32),
            vmem((QUANT, FACES * turn_depth, elems), half),
            vmem((FACES * ghost_all, sides_all), half),
            vmem((QUANT * pair, FACES * ghost_all), half),
        ),
        flops=2 * QUANT * pair * sides_all * sides_all,
        moved=8_000_000,
    )

    (slip_rate,) = call(
        return_kernel,
        "fault_return",
        [Kept(slot_of), Kept(back)],
        [((nodes, faults), f32, "any")],
        flops=2 * pair * slots * faults,
        moved=200_000,
    )
    return dofs_next, slip_rate


def solution(mesh):
    across = ("row", "col")
    placed = (
        P(None, across),
        P(None, across),
        P(None, across),
        P(),
        P(),
        P(),
        P(),
        P(None, across),
        P(None, across),
        P(None, across),
        P(across, None),
        P(across),
        P(None, across),
        P(None, across),
        P(None, across),
        P(None, across),
    )
    return jax.shard_map(
        per_device,
        mesh=mesh,
        in_specs=placed,
        out_specs=(P(None, across), P(None, across)),
        check_vma=False,
    )
```

```python
import jax
import jax.numpy as jnp
from jax import lax
from jax.experimental import pallas as pl
from jax.experimental.pallas import tpu as pltpu
from jax.sharding import PartitionSpec as P

QUANT = 9
ORDER = 6
NEWTON_ITERS = 3
FACES = 4
DIMS = 3
TURNS = 3

time_step = 2.0
fric_a = 0.5
f32 = jnp.float32
half = jnp.bfloat16
MIB = 2**20
LANES = 128
SUB = 8


def up(count, unit):
    return -(-count // unit) * unit


def friction_solve(shear, normal, shear_init, normal_init, state_var, slip_prev):
    shear_total = shear_init + shear
    strength = fric_a * (normal_init * (1.0 + 0.5 * jnp.tanh(normal)))
    growth = jnp.exp(state_var / fric_a) * 0.5
    steep = strength * growth
    slip_now = slip_prev
    for newton_step in range(NEWTON_ITERS):
        scaled = growth * slip_now
        root = jnp.sqrt(1.0 + scaled * scaled)
        positive = jnp.log(jnp.abs(scaled) + root)
        misfit = shear_total - slip_now - strength * jnp.where(scaled < 0.0, -positive, positive)
        slip_now = slip_now + misfit / (1.0 + steep / root)
    return slip_now


def split(values):
    head = values.astype(half).astype(f32)
    return head, values - head


def pad_rows(values, rows):
    if values.shape[0] == rows:
        return values
    return jnp.concatenate(
        [values, jnp.zeros((rows - values.shape[0], values.shape[1]), f32)], axis=0
    )


def pad_lanes(values, lanes):
    if values.shape[1] == lanes:
        return values
    return jnp.concatenate(
        [values, jnp.zeros((values.shape[0], lanes - values.shape[1]), f32)], axis=1
    )


def pieces(values):
    head, rest = split(values)
    return pad_rows(jnp.concatenate([head, rest, head], axis=0), up(3 * values.shape[0], 16)).astype(
        half
    )


def table(values):
    head, rest = split(values)
    return pad_lanes(
        jnp.concatenate([head, head, rest], axis=1), up(3 * values.shape[1], 16)
    ).astype(half)


def product(left, right):
    return jnp.dot(left, right, preferred_element_type=f32)


def lane_row(ref, row, side):
    return ref[row : row + 1, side * LANES : (side + 1) * LANES]


def one_hot(first, rows, index_row):
    places = lax.broadcasted_iota(jnp.int32, (rows, index_row.shape[1]), 0) + first
    return jnp.where(places == index_row, 1.0, 0.0).astype(half)


def flat_row(ref):
    return jnp.concatenate([ref[i : i + 1, :] for i in range(ref.shape[0])], axis=1)


def star_group(star_ref, part_of, side, first, count):
    totals = [None] * count
    for inner in range(QUANT):
        for axis_dir in range(DIMS):
            part = part_of(inner, axis_dir)
            for i in range(count):
                at = (axis_dir * QUANT + first + i) * QUANT + inner
                term = lane_row(star_ref, at, side) * part
                totals[i] = term if totals[i] is None else totals[i] + term
    return totals


def star_apply(star_ref, part_of, side, emit, group=3):
    for first in range(0, QUANT, group):
        for i, total in enumerate(star_group(star_ref, part_of, side, first, group)):
            emit(first + i, total)


def flux_apply(flux_ref, which, values_of, face, side, totals):
    for inner in range(QUANT):
        value = values_of(inner)
        for p in range(QUANT):
            at = ((face * 2 + which) * QUANT + p) * QUANT + inner
            term = lane_row(flux_ref, at, side) * value
            totals[p] = term if totals[p] is None else totals[p] + term
    return totals


class Kept:
    def __init__(self, array):
        self.array = array


class Inputs:
    def __init__(self, sources, targets, sems):
        self.sources, self.targets, self.waiting = sources, targets, {}
        for i, (source, target) in enumerate(zip(sources, targets)):
            if source is target:
                continue
            self.waiting[i] = pltpu.make_async_copy(source, target, sems.at[i])
            self.waiting[i].start()

    def __getitem__(self, i):
        if i in self.waiting:
            self.waiting.pop(i).wait()
        return self.targets[i]

    def rest(self):
        for move in self.waiting.values():
            move.wait()


class Outputs:
    def __init__(self, targets, sources, sems):
        self.targets, self.sources, self.sems = targets, sources, sems
        self.moving = []

    def __getitem__(self, i):
        return self.targets[i] if self.sources[i] is None else self.sources[i]

    def flush(self, i, rows=None):
        source, target = self.sources[i], self.targets[i]
        if source is None:
            return
        if rows is not None:
            source, target = source.at[rows], target.at[rows]
        move = pltpu.make_async_copy(source, target, self.sems.at[len(self.moving)])
        move.start()
        self.moving.append(move)

    def wait(self):
        for move in self.moving:
            move.wait()


def call(kernel, name, ins, outs, scratch=(), flops=0, moved=0, room=32, flushes=None):
    n_in, n_out = len(ins), len(outs)
    placed = [i for i, one in enumerate(outs) if one[2] == "hbm"]
    stays = [isinstance(one, Kept) for one in ins]
    brought = [i for i in range(n_in) if not isinstance(ins[i], Kept)]
    ins = [one.array if isinstance(one, Kept) else one for one in ins]
    flushes = flushes or max(1, len(placed))

    def body(*refs):
        sources, targets = refs[:n_in], refs[n_in : n_in + n_out]
        at = n_in + n_out
        held = list(sources)
        for i in brought:
            held[i], at = refs[at], at + 1
        kept, at = refs[at : at + len(placed)], at + len(placed)
        in_sems, out_sems, *more = refs[at:]
        source_of = [None] * n_out
        for i, ref in zip(placed, kept):
            source_of[i] = ref
        inputs = Inputs(sources, held, in_sems)
        outputs = Outputs(targets, source_of, out_sems)
        kernel(inputs, outputs, *more)
        inputs.rest()
        outputs.wait()

    shapes = [
        {"hbm": pltpu.HBM, "vmem": pltpu.VMEM, "any": jax.ShapeDtypeStruct}[one[2]](one[0], one[1])
        for one in outs
    ]
    spaces = [pltpu.VMEM if one else pltpu.HBM for one in stays]
    return pl.pallas_call(
        body,
        name=name,
        out_shape=shapes,
        in_specs=[pl.BlockSpec(memory_space=space) for space in spaces],
        scratch_shapes=[
            *(pltpu.VMEM(ins[i].shape, ins[i].dtype) for i in brought),
            *(pltpu.VMEM(outs[i][0], outs[i][1]) for i in placed),
            pltpu.SemaphoreType.DMA((max(1, n_in),)),
            pltpu.SemaphoreType.DMA((flushes,)),
            *scratch,
        ],
        cost_estimate=pl.CostEstimate(flops=flops, bytes_accessed=moved, transcendentals=0),
        compiler_params=pltpu.CompilerParams(vmem_limit_bytes=room * MIB),
    )(*(pltpu.with_memory_space_constraint(a, space) for a, space in zip(ins, spaces)))


def per_device(
    dofs,
    star,
    flux_mats,
    kxi,
    face_proj,
    face_lift,
    orient,
    neighbour,
    orient_code,
    send_list,
    fault_part,
    fault_item,
    shear_init,
    normal_init,
    state_var,
    slip_prev,
):
    basis = kxi.shape[1]
    nodes = face_proj.shape[2]
    elems = dofs.shape[1]
    sides = elems // LANES
    ghosts = send_list.shape[1]
    ghost_all = 4 * ghosts
    node_pad = up(nodes, SUB)
    faults = fault_item.shape[0]
    devices = lax.axis_size("row") * lax.axis_size("col")
    slot_most = max(2, 2 * faults // devices)
    slots = devices * slot_most
    sides_all = FACES * elems
    left_q = QUANT // 2
    cut = up(basis // 2, SUB)
    halo_rows = left_q * basis + cut
    depth = up(3 * basis, 16)
    turn_depth = up(3 * node_pad, 16)
    item_row = 4 * node_pad
    pair = 2 * node_pad
    first_q = (0, 3, 6)
    slot_lanes = up(node_pad, 32)
    per_row = LANES // slot_lanes
    chunk = slot_most * slot_lanes
    chunk_shape = (chunk // LANES, LANES) if chunk % LANES == 0 else (chunk,)

    def odd_place():
        return lax.axis_index("row") % 2 == 1, lax.axis_index("col") % 2 == 1

    def predict_kernel(ins, outs, table_ref, chosen_ref, *by_side):
        moved_refs, piece_refs = by_side[:sides], by_side[sides:]
        kxi_at, dofs_at, star_at, part_at, item_at, fault_at, send_at = 0, 1, 2, 3, 4, 5, 9
        asked_at, slot_at, work_at, sends_at = 0, 1, 2, 3
        lanes_of = [slice(side * LANES, (side + 1) * LANES) for side in range(sides)]
        kxi_ref = ins[kxi_at]
        table_ref[...] = table(jnp.concatenate([kxi_ref[d].T for d in range(DIMS)], axis=0))
        dofs_ref, work_ref = ins[dofs_at], outs[work_at]
        for q in range(QUANT):
            rows = slice(q * basis, (q + 1) * basis)
            for side in range(sides):
                start = dofs_ref[rows, lanes_of[side]]
                work_ref[rows, lanes_of[side]] = time_step * start
                piece_refs[side][q] = pieces(start)

        def multiply(side):
            for q in range(0, QUANT, 2):
                quants = range(q, min(q + 2, QUANT))
                right = jnp.concatenate([piece_refs[side][one] for one in quants], axis=1)
                got = product(table_ref[...], right)
                for i, one in enumerate(quants):
                    moved_refs[side][one] = got[:, i * LANES : (i + 1) * LANES]

        def part_of(side):
            return lambda q, d: moved_refs[side][q, d * basis : (d + 1) * basis, :]

        multiply(0)
        by_row = lax.broadcasted_iota(jnp.int32, (faults, faults), 0)
        by_lane = lax.broadcasted_iota(jnp.int32, (faults, faults), 1)
        across = ins[part_at][...]
        wide = jnp.broadcast_to(across, (faults, faults))
        down = jnp.sum(jnp.where(by_row == by_lane, wide, 0), axis=1, keepdims=True)
        rank = jnp.sum(
            jnp.where((down == across) & (by_row < by_lane), 1, 0), axis=0, keepdims=True
        )
        place = across * slot_most + rank
        outs[slot_at][...] = place
        chosen = one_hot(0, slots, place)
        item = (ins[item_at][...] + 1).astype(f32)
        rows = [pad_rows(ins[fault_at + i][...], node_pad) for i in range(4)]
        rows.append(pad_rows(item, LANES - item_row))
        head, rest = split(jnp.concatenate(rows, axis=0))
        outs[asked_at][...] = lax.dot_general(
            jnp.concatenate([chosen, chosen], axis=1),
            jnp.concatenate([head, rest], axis=1).astype(half),
            (((1,), (1,)), ((), ())),
            preferred_element_type=f32,
        )
        outs.flush(asked_at)
        odd_row, odd_col = odd_place()
        picks = ins[send_at][...]
        picks = jnp.concatenate([picks, picks], axis=1)
        order = [
            jnp.where(odd_row, picks[1:2], picks[0:1]),
            jnp.where(odd_row, picks[0:1], picks[1:2]),
            jnp.where(odd_col, picks[3:4], picks[2:3]),
            jnp.where(odd_col, picks[2:3], picks[3:4]),
        ]
        width = 2 * ghosts
        for d in range(4):
            chosen_ref[:, d * width : (d + 1) * width] = one_hot(0, elems, order[d])
        star_ref = ins[star_at]

        def advance(order_k, factor):
            factor = factor * time_step / (order_k + 1).astype(f32)
            for side in range(sides):
                lanes = lanes_of[side]

                def emit(p, value):
                    piece_refs[side][p] = pieces(value)
                    rows = slice(p * basis, (p + 1) * basis)
                    work_ref[rows, lanes] = work_ref[rows, lanes] + factor * value

                multiply((side + 1) % sides)
                star_apply(star_ref, part_of(side), side, emit)
            return factor

        factor = lax.fori_loop(1, ORDER - 1, advance, f32(time_step))
        factor = factor * (time_step / ORDER)

        for side in range(sides):
            lanes = lanes_of[side]

            def emit_last(p, value):
                rows = slice(p * basis, (p + 1) * basis)
                work_ref[rows, lanes] = work_ref[rows, lanes] + factor * value

            if side + 1 < sides:
                multiply(side + 1)
            star_apply(star_ref, part_of(side), side, emit_last)
        heads, rests = split(work_ref[...])
        both = product(jnp.concatenate([heads, rests], axis=0).astype(half), chosen_ref[...])
        got = both[: QUANT * basis] + both[QUANT * basis :]
        right = pad_rows(got[halo_rows:], halo_rows)
        low = lax.broadcasted_iota(jnp.int32, (halo_rows, width), 1) < ghosts
        for d in range(4):
            lanes = slice(d * width, (d + 1) * width)
            outs[sends_at + d][...] = jnp.where(low, got[:halo_rows, lanes], right[:, lanes])

    def asked_item(asked):
        return asked[item_row : item_row + 1, :].astype(jnp.int32) - 1

    def local_kernel(ins, outs, left_ref, chosen_ref, wanted_ref):
        proj_at, near_at, work_at, orient_at, code_at, asked_at = range(6)
        seen_at, fric_at, slot_seen_at, slot_near_at, slot_code_at = range(5)
        trace_table_at, turn_table_at, near_out, code_out = range(5, 9)
        proj_ref = ins[proj_at]
        trace_table = table(
            jnp.concatenate([pad_rows(proj_ref[:, j, :], node_pad) for j in range(FACES)], axis=0)
        )
        outs[trace_table_at][...] = trace_table
        work_ref = ins[work_at]
        kept = {}
        for q in range(QUANT):
            got = product(trace_table, pieces(work_ref[q * basis : (q + 1) * basis, :]))
            if q in first_q:
                kept[q] = got
            for j in range(FACES):
                head, rest = split(got[j * node_pad : (j + 1) * node_pad])
                left_ref[q * pair : (q + 1) * pair, j * elems : (j + 1) * elems] = jnp.concatenate(
                    [head, rest], axis=0
                ).astype(half)
        near = flat_row(ins[near_at])
        odd_row, odd_col = odd_place()
        block = (near // ghosts) % 4
        flip = jnp.where(block < 2, jnp.where(odd_row, 0, 1), jnp.where(odd_col, 0, 1))
        near = jnp.where(near < sides_all, near, near + ghosts * flip * (1 - 2 * (block % 2)))
        outs[near_out][...] = near
        code = flat_row(ins[code_at])
        outs[code_out][...] = code
        orient_ref = ins[orient_at]
        outs[turn_table_at][...] = table(
            jnp.concatenate(
                [pad_lanes(pad_rows(orient_ref[t].T, node_pad), node_pad) for t in range(TURNS)],
                axis=0,
            )
        )
        for j in range(FACES):
            chosen_ref[j * elems : (j + 1) * elems, :] = one_hot(j * elems, elems, near)
        outs[seen_at][...] = product(left_ref[...], chosen_ref[...]).astype(half)
        item = asked_item(ins[asked_at][...].T)
        wanted_ref[...] = one_hot(0, sides_all, item)
        near_head, near_rest = split(near.astype(f32))
        shear, normal = [], []
        for j in range(FACES):
            rows = slice(j * node_pad, (j + 1) * node_pad)
            shear.append(0.5 * (kept[3][rows] + kept[6][rows]))
            normal.append(0.5 * kept[0][rows])
        rows = [*split(jnp.concatenate(shear, axis=1)), *split(jnp.concatenate(normal, axis=1))]
        rows += [near_head, near_rest, code.astype(f32)]
        rows = jnp.concatenate(rows, axis=0)
        taken = product(pad_rows(rows, up(rows.shape[0], 16)).astype(half), wanted_ref[...])
        outs[fric_at][:node_pad, :] = taken[:node_pad] + taken[node_pad:pair]
        outs[fric_at][node_pad:, :] = taken[pair : pair + node_pad] + taken[pair + node_pad : 2 * pair]
        slot_near = (taken[2 * pair : 2 * pair + 1] + taken[2 * pair + 1 : 2 * pair + 2]).astype(jnp.int32)
        slot_near = jnp.where(item < 0, -1, slot_near)
        outs[slot_near_at][...] = slot_near
        outs[slot_code_at][...] = taken[2 * pair + 2 : 2 * pair + 3].astype(jnp.int32)
        left = jnp.concatenate([left_ref[q * pair : (q + 1) * pair, :] for q in first_q], axis=0)
        outs[slot_seen_at][...] = product(left, one_hot(0, sides_all, slot_near)).astype(half)

    def seen_across(
        got_refs, quants, trace_table, turn_table, near, code, seen_ref, chosen_ref, left_ref, emit
    ):
        def joined(first, second, begin, end):
            low = lax.broadcasted_iota(jnp.int32, (end - begin, 2 * ghosts), 1) < ghosts
            if end <= halo_rows:
                rows = slice(begin, end)
                return jnp.where(low, first[rows, :], pltpu.roll(second[rows, :], ghosts, 1))
            rows = slice(begin - halo_rows, end - halo_rows)
            return jnp.where(low, pltpu.roll(first[rows, :], ghosts, 1), second[rows, :])

        def ghost_rows(first, second, begin, end):
            if begin < halo_rows < end:
                parts = [joined(first, second, begin, halo_rows), joined(first, second, halo_rows, end)]
                return jnp.concatenate(parts, axis=0)
            return joined(first, second, begin, end)

        for j in range(FACES):
            chosen_ref[j * ghost_all : (j + 1) * ghost_all, :] = one_hot(
                sides_all + j * ghost_all, ghost_all, near
            )
        for at, q in enumerate(quants):
            halves = [
                ghost_rows(first, second, q * basis, (q + 1) * basis)
                for first, second in (got_refs[:2], got_refs[2:])
            ]
            got = product(trace_table, pieces(jnp.concatenate(halves, axis=1)))
            for j in range(FACES):
                head, rest = split(got[j * node_pad : (j + 1) * node_pad])
                left_ref[
                    at * pair : (at + 1) * pair, j * ghost_all : (j + 1) * ghost_all
                ] = jnp.concatenate([head, rest], axis=0).astype(half)
        found = product(left_ref[...], chosen_ref[...])
        is_zero = jnp.broadcast_to(code, (node_pad, code.shape[1])) == 0
        is_one = jnp.broadcast_to(code, (node_pad, code.shape[1])) == 1
        for at, q in enumerate(quants):
            both = found[at * pair : (at + 1) * pair]
            both = both + seen_ref[at * pair : (at + 1) * pair].astype(f32)
            right = pad_rows(jnp.concatenate([both, both[:node_pad]], axis=0), turn_depth)
            rotated = product(turn_table, right.astype(half))
            emit(
                q,
                jnp.where(
                    is_zero,
                    rotated[:node_pad],
                    jnp.where(is_one, rotated[node_pad : 2 * node_pad], rotated[2 * node_pad :]),
                ),
            )

    def friction_kernel(ins, outs, chosen_ref, left_ref, wide_ref):
        got_at = range(4)
        trace_table_at, turn_table_at, near_at, code_at, seen_at, fric_at, asked_at = range(4, 11)
        back_at, slip_at = range(2)
        kept = {}

        def emit(q, value):
            kept[q] = value

        seen_across(
            [ins[i] for i in got_at],
            first_q,
            ins[trace_table_at][...],
            ins[turn_table_at][...],
            ins[near_at][...],
            ins[code_at][...],
            ins[seen_at],
            chosen_ref,
            left_ref,
            emit,
        )
        fric_ref = ins[fric_at]
        asked = ins[asked_at][...].T
        own = [asked[i * node_pad : (i + 1) * node_pad] for i in range(4)]
        slip = friction_solve(
            fric_ref[:node_pad, :] + 0.5 * (kept[3] - kept[6]),
            fric_ref[node_pad:, :] + 0.5 * kept[0],
            *own,
        )
        wide_ref[...] = pad_rows(slip, LANES).T
        packed = wide_ref[pl.ds(0, slots // per_row, stride=per_row), :]
        for k in range(1, per_row):
            part = wide_ref[pl.ds(k, slots // per_row, stride=per_row), :]
            packed = packed + pltpu.roll(part, k * slot_lanes, 1)
        outs[back_at][...] = packed
        outs[slip_at][...] = slip
        outs.flush(slip_at)

    def final_kernel(ins, outs, moved_ref, trace_ref, turned_ref, mixed_ref, chosen_ref, left_ref):
        got_at = range(4)
        trace_table_at, turn_table_at, near_at, code_at, seen_at, asked_at, slip_at = range(4, 11)
        work_at, lift_at, kxi_at, flux_at, star_at, dofs_at = range(11, 17)

        def emit(q, value):
            turned_ref[q * node_pad : (q + 1) * node_pad, :] = value

        seen_across(
            [ins[i] for i in got_at],
            range(QUANT),
            ins[trace_table_at][...],
            ins[turn_table_at][...],
            ins[near_at][...],
            ins[code_at][...],
            ins[seen_at],
            chosen_ref,
            left_ref,
            emit,
        )
        asked = ins[asked_at][...].T
        wanted = one_hot(0, sides_all, asked_item(asked))
        slip_head, slip_rest = split(ins[slip_at][...])
        pushed = lax.dot_general(
            jnp.concatenate([slip_head, slip_rest], axis=0).astype(half),
            wanted,
            (((1,), (1,)), ((), ())),
            preferred_element_type=f32,
        )
        pushed = 2.0 * (pushed[:node_pad] + pushed[node_pad:])
        kxi_ref, lift_ref, work_ref = ins[kxi_at], ins[lift_at], ins[work_at]
        back_table = table(jnp.concatenate([kxi_ref[d] for d in range(DIMS)], axis=0))
        lift_table = jnp.concatenate(
            [table(pad_lanes(lift_ref[:, j, :].T, node_pad)) for j in range(FACES)], axis=1
        )
        trace_table = ins[trace_table_at][...]
        for q in range(QUANT):
            right = pieces(work_ref[q * basis : (q + 1) * basis, :])
            moved_ref[q] = product(back_table, right)
            trace_ref[q] = product(trace_table, right)
        flux_ref = ins[flux_at]
        for side in range(sides):
            lanes = slice(side * LANES, (side + 1) * LANES)
            for j in range(FACES):
                at = j * elems + side * LANES
                totals = flux_apply(
                    flux_ref,
                    0,
                    lambda q: trace_ref[q, j * node_pad : (j + 1) * node_pad, lanes],
                    j,
                    side,
                    [None] * QUANT,
                )
                totals = flux_apply(
                    flux_ref,
                    1,
                    lambda q: turned_ref[q * node_pad : (q + 1) * node_pad, at : at + LANES],
                    j,
                    side,
                    totals,
                )
                push = pushed[:, at : at + LANES]
                totals[3] = totals[3] - push
                totals[6] = totals[6] + push
                for p in range(QUANT):
                    mixed_ref[p, j * turn_depth : (j + 1) * turn_depth, lanes] = pieces(totals[p])
        star_ref, dofs_ref = ins[star_at], ins[dofs_at]
        out_ref = outs[0]
        for side in range(sides):
            lanes = slice(side * LANES, (side + 1) * LANES)

            def emit(p, value):
                rows = slice(p * basis, (p + 1) * basis)
                out_ref[rows, lanes] = dofs_ref[rows, lanes] + 0.25 * value

            star_apply(
                star_ref,
                lambda q, d: moved_ref[q, d * basis : (d + 1) * basis, lanes],
                side,
                emit,
            )
        for p in range(QUANT):
            rows = slice(p * basis, (p + 1) * basis)
            out_ref[rows, :] = out_ref[rows, :] + 0.25 * product(lift_table, mixed_ref[p])

    def return_kernel(ins, outs):
        place = ins[0][...]
        held = ins[1][...].T
        rows = slots // per_row
        got = jnp.zeros((pair, faults), f32)
        for k in range(per_row):
            head, rest = split(held[k * slot_lanes : k * slot_lanes + node_pad])
            chosen = one_hot(0, rows, jnp.where(place % per_row == k, place // per_row, -1))
            got = got + product(jnp.concatenate([head, rest], axis=0).astype(half), chosen)
        outs[0][...] = (got[:node_pad] + got[node_pad:])[:nodes]

    vmem = pltpu.VMEM
    proj_rows = jnp.transpose(face_proj, (2, 0, 1))
    lift_rows = jnp.transpose(face_lift, (1, 0, 2))
    asked, slot_of, work, *sends = call(
        predict_kernel,
        "predict",
        [
            kxi,
            dofs,
            star,
            fault_part.reshape(1, faults),
            fault_item.reshape(1, faults),
            shear_init,
            normal_init,
            state_var,
            slip_prev,
            send_list,
        ],
        [
            ((slots, LANES), f32, "hbm"),
            ((1, faults), jnp.int32, "vmem"),
            (dofs.shape, f32, "vmem"),
        ]
        + [((halo_rows, 2 * ghosts), f32, "any")] * 4,
        scratch=(
            vmem((DIMS * basis, depth), half),
            vmem((elems, 8 * ghosts), half),
            *[vmem((QUANT, DIMS * basis, LANES), f32)] * sides,
            *[vmem((QUANT, depth, LANES), half)] * sides,
        ),
        flops=5 * 2 * DIMS * basis * depth * QUANT * elems,
        moved=8_000_000,
    )

    asked = lax.all_to_all(
        asked.reshape(devices, slot_most, LANES), ("row", "col"), split_axis=0, concat_axis=0, tiled=True
    ).reshape(slots, LANES)

    def swapped(values, axis, first):
        pairs = [(i, i + 1) for i in range(first, lax.axis_size(axis) - 1, 2)]
        return lax.ppermute(values, axis, pairs + [(b, a) for a, b in pairs])

    arrived = [
        swapped(sends[0], "row", 0),
        swapped(sends[1], "row", 1),
        swapped(sends[2], "col", 0),
        swapped(sends[3], "col", 1),
    ]

    seen, fric, slot_seen, slot_near, slot_code, trace_table, turn_table, near, code = call(
        local_kernel,
        "local_terms",
        [proj_rows, neighbour, Kept(work), orient, orient_code, Kept(asked)],
        [
            ((QUANT * pair, sides_all), half, "vmem"),
            ((pair, slots), f32, "vmem"),
            ((len(first_q) * pair, slots), half, "vmem"),
            ((1, slots), jnp.int32, "vmem"),
            ((1, slots), jnp.int32, "vmem"),
            ((FACES * node_pad, depth), half, "vmem"),
            ((TURNS * node_pad, turn_depth), half, "vmem"),
            ((1, sides_all), jnp.int32, "vmem"),
            ((1, sides_all), jnp.int32, "vmem"),
        ],
        scratch=(
            vmem((QUANT * pair, sides_all), half),
            vmem((sides_all, sides_all), half),
            vmem((sides_all, slots), half),
        ),
        flops=2 * QUANT * pair * sides_all * sides_all,
        moved=8_000_000,
    )

    back, slip = call(
        friction_kernel,
        "friction",
        [
            Kept(one)
            for one in (*arrived, trace_table, turn_table, slot_near, slot_code, slot_seen, fric, asked)
        ],
        [((slots // per_row, LANES), f32, "any"), ((node_pad, slots), f32, "vmem")],
        scratch=(
            vmem((FACES * ghost_all, slots), half),
            vmem((len(first_q) * pair, FACES * ghost_all), half),
            vmem((slots, LANES), f32),
        ),
        flops=2 * len(first_q) * pair * sides_all * slots,
        moved=4_000_000,
    )
    back = lax.all_to_all(
        back.reshape(devices, *chunk_shape), ("row", "col"), split_axis=0, concat_axis=0, tiled=True
    ).reshape(slots // per_row, LANES)

    (dofs_next,) = call(
        final_kernel,
        "final_terms",
        [
            *(Kept(one) for one in arrived),
            Kept(trace_table),
            Kept(turn_table),
            Kept(near),
            Kept(code),
            Kept(seen),
            Kept(asked),
            Kept(slip),
            Kept(work),
            lift_rows,
            kxi,
            flux_mats,
            star,
            dofs,
        ],
        [(dofs.shape, f32, "any")],
        scratch=(
            vmem((QUANT, DIMS * basis, elems), f32),
            vmem((QUANT, FACES * node_pad, elems), f32),
            vmem((QUANT * node_pad, sides_all), f32),
            vmem((QUANT, FACES * turn_depth, elems), half),
            vmem((FACES * ghost_all, sides_all), half),
            vmem((QUANT * pair, FACES * ghost_all), half),
        ),
        flops=2 * QUANT * pair * sides_all * sides_all,
        moved=8_000_000,
    )

    (slip_rate,) = call(
        return_kernel,
        "fault_return",
        [Kept(slot_of), Kept(back)],
        [((nodes, faults), f32, "any")],
        flops=2 * pair * slots * faults,
        moved=200_000,
    )
    return dofs_next, slip_rate


def solution(mesh):
    across = ("row", "col")
    placed = (
        P(None, across),
        P(None, across),
        P(None, across),
        P(),
        P(),
        P(),
        P(),
        P(None, across),
        P(None, across),
        P(None, across),
        P(across, None),
        P(across),
        P(None, across),
        P(None, across),
        P(None, across),
        P(None, across),
    )
    return jax.shard_map(
        per_device,
        mesh=mesh,
        in_specs=placed,
        out_specs=(P(None, across), P(None, across)),
        check_vma=False,
    )
```

```python
import jax
import jax.numpy as jnp
from jax import lax
from jax.experimental import pallas as pl
from jax.experimental.pallas import tpu as pltpu
from jax.sharding import PartitionSpec as P

QUANT = 9
ORDER = 6
NEWTON_ITERS = 3
FACES = 4
DIMS = 3
TURNS = 3

time_step = 2.0
fric_a = 0.5
f32 = jnp.float32
half = jnp.bfloat16
MIB = 2**20
LANES = 128
SUB = 8


def up(count, unit):
    return -(-count // unit) * unit


def friction_solve(shear, normal, shear_init, normal_init, state_var, slip_prev):
    shear_total = shear_init + shear
    strength = fric_a * (normal_init * (1.0 + 0.5 * jnp.tanh(normal)))
    growth = jnp.exp(state_var / fric_a) * 0.5
    steep = strength * growth
    slip_now = slip_prev
    for newton_step in range(NEWTON_ITERS):
        scaled = growth * slip_now
        root = jnp.sqrt(1.0 + scaled * scaled)
        positive = jnp.log(jnp.abs(scaled) + root)
        misfit = shear_total - slip_now - strength * jnp.where(scaled < 0.0, -positive, positive)
        slip_now = slip_now + misfit / (1.0 + steep / root)
    return slip_now


def split(values):
    head = values.astype(half).astype(f32)
    return head, values - head


def pad_rows(values, rows):
    if values.shape[0] == rows:
        return values
    return jnp.concatenate(
        [values, jnp.zeros((rows - values.shape[0], values.shape[1]), f32)], axis=0
    )


def pad_lanes(values, lanes):
    if values.shape[1] == lanes:
        return values
    return jnp.concatenate(
        [values, jnp.zeros((values.shape[0], lanes - values.shape[1]), f32)], axis=1
    )


def pieces(values):
    head, rest = split(values)
    return pad_rows(jnp.concatenate([head, rest, head], axis=0), up(3 * values.shape[0], 16)).astype(
        half
    )


def table(values):
    head, rest = split(values)
    return pad_lanes(
        jnp.concatenate([head, head, rest], axis=1), up(3 * values.shape[1], 16)
    ).astype(half)


def product(left, right):
    return jnp.dot(left, right, preferred_element_type=f32)


def lane_row(ref, row, side):
    return ref[row : row + 1, side * LANES : (side + 1) * LANES]


def one_hot(first, rows, index_row):
    places = lax.broadcasted_iota(jnp.int32, (rows, index_row.shape[1]), 0) + first
    return jnp.where(places == index_row, 1.0, 0.0).astype(half)


def flat_row(ref):
    return jnp.concatenate([ref[i : i + 1, :] for i in range(ref.shape[0])], axis=1)


def star_group(star_ref, part_of, side, first, count):
    totals = [None] * count
    for inner in range(QUANT):
        for axis_dir in range(DIMS):
            part = part_of(inner, axis_dir)
            for i in range(count):
                at = (axis_dir * QUANT + first + i) * QUANT + inner
                term = lane_row(star_ref, at, side) * part
                totals[i] = term if totals[i] is None else totals[i] + term
    return totals


def star_apply(star_ref, part_of, side, emit, group=3):
    for first in range(0, QUANT, group):
        for i, total in enumerate(star_group(star_ref, part_of, side, first, group)):
            emit(first + i, total)


def flux_apply(flux_ref, which, values_of, face, side, totals):
    for inner in range(QUANT):
        value = values_of(inner)
        for p in range(QUANT):
            at = ((face * 2 + which) * QUANT + p) * QUANT + inner
            term = lane_row(flux_ref, at, side) * value
            totals[p] = term if totals[p] is None else totals[p] + term
    return totals


class Kept:
    def __init__(self, array):
        self.array = array


class Inputs:
    def __init__(self, sources, targets, sems):
        self.sources, self.targets, self.waiting = sources, targets, {}
        for i, (source, target) in enumerate(zip(sources, targets)):
            if source is target:
                continue
            self.waiting[i] = pltpu.make_async_copy(source, target, sems.at[i])
            self.waiting[i].start()

    def __getitem__(self, i):
        if i in self.waiting:
            self.waiting.pop(i).wait()
        return self.targets[i]

    def rest(self):
        for move in self.waiting.values():
            move.wait()


class Outputs:
    def __init__(self, targets, sources, sems):
        self.targets, self.sources, self.sems = targets, sources, sems
        self.moving = []

    def __getitem__(self, i):
        return self.targets[i] if self.sources[i] is None else self.sources[i]

    def flush(self, i, rows=None):
        source, target = self.sources[i], self.targets[i]
        if source is None:
            return
        if rows is not None:
            source, target = source.at[rows], target.at[rows]
        move = pltpu.make_async_copy(source, target, self.sems.at[len(self.moving)])
        move.start()
        self.moving.append(move)

    def wait(self):
        for move in self.moving:
            move.wait()


def call(kernel, name, ins, outs, scratch=(), flops=0, moved=0, room=32, flushes=None):
    n_in, n_out = len(ins), len(outs)
    placed = [i for i, one in enumerate(outs) if one[2] == "hbm"]
    stays = [isinstance(one, Kept) for one in ins]
    brought = [i for i in range(n_in) if not isinstance(ins[i], Kept)]
    ins = [one.array if isinstance(one, Kept) else one for one in ins]
    flushes = flushes or max(1, len(placed))

    def body(*refs):
        sources, targets = refs[:n_in], refs[n_in : n_in + n_out]
        at = n_in + n_out
        held = list(sources)
        for i in brought:
            held[i], at = refs[at], at + 1
        kept, at = refs[at : at + len(placed)], at + len(placed)
        in_sems, out_sems, *more = refs[at:]
        source_of = [None] * n_out
        for i, ref in zip(placed, kept):
            source_of[i] = ref
        inputs = Inputs(sources, held, in_sems)
        outputs = Outputs(targets, source_of, out_sems)
        kernel(inputs, outputs, *more)
        inputs.rest()
        outputs.wait()

    shapes = [
        {"hbm": pltpu.HBM, "vmem": pltpu.VMEM, "any": jax.ShapeDtypeStruct}[one[2]](one[0], one[1])
        for one in outs
    ]
    spaces = [pltpu.VMEM if one else pltpu.HBM for one in stays]
    return pl.pallas_call(
        body,
        name=name,
        out_shape=shapes,
        in_specs=[pl.BlockSpec(memory_space=space) for space in spaces],
        scratch_shapes=[
            *(pltpu.VMEM(ins[i].shape, ins[i].dtype) for i in brought),
            *(pltpu.VMEM(outs[i][0], outs[i][1]) for i in placed),
            pltpu.SemaphoreType.DMA((max(1, n_in),)),
            pltpu.SemaphoreType.DMA((flushes,)),
            *scratch,
        ],
        cost_estimate=pl.CostEstimate(flops=flops, bytes_accessed=moved, transcendentals=0),
        compiler_params=pltpu.CompilerParams(vmem_limit_bytes=room * MIB),
    )(*(pltpu.with_memory_space_constraint(a, space) for a, space in zip(ins, spaces)))


def per_device(
    dofs,
    star,
    flux_mats,
    kxi,
    face_proj,
    face_lift,
    orient,
    neighbour,
    orient_code,
    send_list,
    fault_part,
    fault_item,
    shear_init,
    normal_init,
    state_var,
    slip_prev,
):
    basis = kxi.shape[1]
    nodes = face_proj.shape[2]
    elems = dofs.shape[1]
    sides = elems // LANES
    ghosts = send_list.shape[1]
    ghost_all = 4 * ghosts
    node_pad = up(nodes, SUB)
    faults = fault_item.shape[0]
    devices = lax.axis_size("row") * lax.axis_size("col")
    slot_most = max(2, 2 * faults // devices)
    slots = devices * slot_most
    sides_all = FACES * elems
    left_q = QUANT // 2
    cut = up(basis // 2, SUB)
    halo_rows = left_q * basis + cut
    depth = up(3 * basis, 16)
    turn_depth = up(3 * node_pad, 16)
    item_row = 4 * node_pad
    pair = 2 * node_pad
    first_q = (0, 3, 6)
    slot_lanes = up(node_pad, 32)
    per_row = LANES // slot_lanes
    chunk = slot_most * slot_lanes
    chunk_shape = (chunk // LANES, LANES) if chunk % LANES == 0 else (chunk,)

    def odd_place():
        return lax.axis_index("row") % 2 == 1, lax.axis_index("col") % 2 == 1

    def predict_kernel(ins, outs, table_ref, chosen_ref, *by_side):
        moved_refs, piece_refs = by_side[:sides], by_side[sides:]
        kxi_at, dofs_at, star_at, part_at, item_at, fault_at, send_at = 0, 1, 2, 3, 4, 5, 9
        asked_at, slot_at, work_at, sends_at = 0, 1, 2, 3
        lanes_of = [slice(side * LANES, (side + 1) * LANES) for side in range(sides)]
        kxi_ref = ins[kxi_at]
        table_ref[...] = table(jnp.concatenate([kxi_ref[d].T for d in range(DIMS)], axis=0))
        dofs_ref, work_ref = ins[dofs_at], outs[work_at]
        for q in range(QUANT):
            rows = slice(q * basis, (q + 1) * basis)
            for side in range(sides):
                start = dofs_ref[rows, lanes_of[side]]
                work_ref[rows, lanes_of[side]] = time_step * start
                piece_refs[side][q] = pieces(start)

        def multiply(side):
            for q in range(0, QUANT, 2):
                quants = range(q, min(q + 2, QUANT))
                right = jnp.concatenate([piece_refs[side][one] for one in quants], axis=1)
                got = product(table_ref[...], right)
                for i, one in enumerate(quants):
                    moved_refs[side][one] = got[:, i * LANES : (i + 1) * LANES]

        def part_of(side):
            return lambda q, d: moved_refs[side][q, d * basis : (d + 1) * basis, :]

        multiply(0)
        by_row = lax.broadcasted_iota(jnp.int32, (faults, faults), 0)
        by_lane = lax.broadcasted_iota(jnp.int32, (faults, faults), 1)
        across = ins[part_at][...]
        wide = jnp.broadcast_to(across, (faults, faults))
        down = jnp.sum(jnp.where(by_row == by_lane, wide, 0), axis=1, keepdims=True)
        rank = jnp.sum(
            jnp.where((down == across) & (by_row < by_lane), 1, 0), axis=0, keepdims=True
        )
        place = across * slot_most + rank
        outs[slot_at][...] = place
        chosen = one_hot(0, slots, place)
        item = (ins[item_at][...] + 1).astype(f32)
        rows = [pad_rows(ins[fault_at + i][...], node_pad) for i in range(4)]
        rows.append(pad_rows(item, LANES - item_row))
        head, rest = split(jnp.concatenate(rows, axis=0))
        outs[asked_at][...] = lax.dot_general(
            jnp.concatenate([chosen, chosen], axis=1),
            jnp.concatenate([head, rest], axis=1).astype(half),
            (((1,), (1,)), ((), ())),
            preferred_element_type=f32,
        )
        outs.flush(asked_at)
        odd_row, odd_col = odd_place()
        picks = ins[send_at][...]
        picks = jnp.concatenate([picks, picks], axis=1)
        order = [
            jnp.where(odd_row, picks[1:2], picks[0:1]),
            jnp.where(odd_row, picks[0:1], picks[1:2]),
            jnp.where(odd_col, picks[3:4], picks[2:3]),
            jnp.where(odd_col, picks[2:3], picks[3:4]),
        ]
        width = 2 * ghosts
        for d in range(4):
            chosen_ref[:, d * width : (d + 1) * width] = one_hot(0, elems, order[d])
        star_ref = ins[star_at]

        def advance(order_k, factor):
            factor = factor * time_step / (order_k + 1).astype(f32)
            for side in range(sides):
                lanes = lanes_of[side]

                def emit(p, value):
                    piece_refs[side][p] = pieces(value)
                    rows = slice(p * basis, (p + 1) * basis)
                    work_ref[rows, lanes] = work_ref[rows, lanes] + factor * value

                multiply((side + 1) % sides)
                star_apply(star_ref, part_of(side), side, emit)
            return factor

        factor = lax.fori_loop(1, ORDER - 1, advance, f32(time_step))
        factor = factor * (time_step / ORDER)

        for side in range(sides):
            lanes = lanes_of[side]

            def emit_last(p, value):
                rows = slice(p * basis, (p + 1) * basis)
                work_ref[rows, lanes] = work_ref[rows, lanes] + factor * value

            if side + 1 < sides:
                multiply(side + 1)
            star_apply(star_ref, part_of(side), side, emit_last)
        heads, rests = split(work_ref[...])
        both = product(jnp.concatenate([heads, rests], axis=0).astype(half), chosen_ref[...])
        got = both[: QUANT * basis] + both[QUANT * basis :]
        right = pad_rows(got[halo_rows:], halo_rows)
        low = lax.broadcasted_iota(jnp.int32, (halo_rows, width), 1) < ghosts
        for d in range(4):
            lanes = slice(d * width, (d + 1) * width)
            outs[sends_at + d][...] = jnp.where(low, got[:halo_rows, lanes], right[:, lanes])

    def asked_item(asked):
        return asked[item_row : item_row + 1, :].astype(jnp.int32) - 1

    def local_kernel(ins, outs, left_ref, chosen_ref, wanted_ref):
        proj_at, near_at, work_at, orient_at, code_at, asked_at = range(6)
        seen_at, fric_at, slot_seen_at, slot_near_at, slot_code_at = range(5)
        trace_table_at, turn_table_at, near_out, code_out = range(5, 9)
        proj_ref = ins[proj_at]
        trace_table = table(
            jnp.concatenate([pad_rows(proj_ref[:, j, :], node_pad) for j in range(FACES)], axis=0)
        )
        outs[trace_table_at][...] = trace_table
        work_ref = ins[work_at]
        kept = {}
        for q in range(QUANT):
            got = product(trace_table, pieces(work_ref[q * basis : (q + 1) * basis, :]))
            if q in first_q:
                kept[q] = got
            for j in range(FACES):
                head, rest = split(got[j * node_pad : (j + 1) * node_pad])
                left_ref[q * pair : (q + 1) * pair, j * elems : (j + 1) * elems] = jnp.concatenate(
                    [head, rest], axis=0
                ).astype(half)
        near = flat_row(ins[near_at])
        odd_row, odd_col = odd_place()
        block = (near // ghosts) % 4
        flip = jnp.where(block < 2, jnp.where(odd_row, 0, 1), jnp.where(odd_col, 0, 1))
        near = jnp.where(near < sides_all, near, near + ghosts * flip * (1 - 2 * (block % 2)))
        outs[near_out][...] = near
        code = flat_row(ins[code_at])
        outs[code_out][...] = code
        orient_ref = ins[orient_at]
        outs[turn_table_at][...] = table(
            jnp.concatenate(
                [pad_lanes(pad_rows(orient_ref[t].T, node_pad), node_pad) for t in range(TURNS)],
                axis=0,
            )
        )
        for j in range(FACES):
            chosen_ref[j * elems : (j + 1) * elems, :] = one_hot(j * elems, elems, near)
        outs[seen_at][...] = product(left_ref[...], chosen_ref[...]).astype(half)
        item = asked_item(ins[asked_at][...].T)
        wanted_ref[...] = one_hot(0, sides_all, item)
        near_head, near_rest = split(near.astype(f32))
        shear, normal = [], []
        for j in range(FACES):
            rows = slice(j * node_pad, (j + 1) * node_pad)
            shear.append(0.5 * (kept[3][rows] + kept[6][rows]))
            normal.append(0.5 * kept[0][rows])
        rows = [*split(jnp.concatenate(shear, axis=1)), *split(jnp.concatenate(normal, axis=1))]
        rows += [near_head, near_rest, code.astype(f32)]
        rows = jnp.concatenate(rows, axis=0)
        taken = product(pad_rows(rows, up(rows.shape[0], 16)).astype(half), wanted_ref[...])
        outs[fric_at][:node_pad, :] = taken[:node_pad] + taken[node_pad:pair]
        outs[fric_at][node_pad:, :] = taken[pair : pair + node_pad] + taken[pair + node_pad : 2 * pair]
        slot_near = (taken[2 * pair : 2 * pair + 1] + taken[2 * pair + 1 : 2 * pair + 2]).astype(jnp.int32)
        slot_near = jnp.where(item < 0, -1, slot_near)
        outs[slot_near_at][...] = slot_near
        outs[slot_code_at][...] = taken[2 * pair + 2 : 2 * pair + 3].astype(jnp.int32)
        left = jnp.concatenate([left_ref[q * pair : (q + 1) * pair, :] for q in first_q], axis=0)
        outs[slot_seen_at][...] = product(left, one_hot(0, sides_all, slot_near)).astype(half)

    def seen_across(
        got_refs, quants, trace_table, turn_table, near, code, seen_ref, chosen_ref, left_ref, emit
    ):
        def joined(first, second, begin, end):
            low = lax.broadcasted_iota(jnp.int32, (end - begin, 2 * ghosts), 1) < ghosts
            if end <= halo_rows:
                rows = slice(begin, end)
                return jnp.where(low, first[rows, :], pltpu.roll(second[rows, :], ghosts, 1))
            rows = slice(begin - halo_rows, end - halo_rows)
            return jnp.where(low, pltpu.roll(first[rows, :], ghosts, 1), second[rows, :])

        def ghost_rows(first, second, begin, end):
            if begin < halo_rows < end:
                parts = [joined(first, second, begin, halo_rows), joined(first, second, halo_rows, end)]
                return jnp.concatenate(parts, axis=0)
            return joined(first, second, begin, end)

        for j in range(FACES):
            chosen_ref[j * ghost_all : (j + 1) * ghost_all, :] = one_hot(
                sides_all + j * ghost_all, ghost_all, near
            )
        for at, q in enumerate(quants):
            halves = [
                ghost_rows(first, second, q * basis, (q + 1) * basis)
                for first, second in (got_refs[:2], got_refs[2:])
            ]
            got = product(trace_table, pieces(jnp.concatenate(halves, axis=1)))
            for j in range(FACES):
                head, rest = split(got[j * node_pad : (j + 1) * node_pad])
                left_ref[
                    at * pair : (at + 1) * pair, j * ghost_all : (j + 1) * ghost_all
                ] = jnp.concatenate([head, rest], axis=0).astype(half)
        found = product(left_ref[...], chosen_ref[...])
        is_zero = jnp.broadcast_to(code, (node_pad, code.shape[1])) == 0
        is_one = jnp.broadcast_to(code, (node_pad, code.shape[1])) == 1
        for at, q in enumerate(quants):
            both = found[at * pair : (at + 1) * pair]
            both = both + seen_ref[at * pair : (at + 1) * pair].astype(f32)
            right = pad_rows(jnp.concatenate([both, both[:node_pad]], axis=0), turn_depth)
            rotated = product(turn_table, right.astype(half))
            emit(
                q,
                jnp.where(
                    is_zero,
                    rotated[:node_pad],
                    jnp.where(is_one, rotated[node_pad : 2 * node_pad], rotated[2 * node_pad :]),
                ),
            )

    def friction_kernel(ins, outs, chosen_ref, left_ref, wide_ref):
        got_at = range(4)
        trace_table_at, turn_table_at, near_at, code_at, seen_at, fric_at, asked_at = range(4, 11)
        back_at, slip_at = range(2)
        kept = {}

        def emit(q, value):
            kept[q] = value

        seen_across(
            [ins[i] for i in got_at],
            first_q,
            ins[trace_table_at][...],
            ins[turn_table_at][...],
            ins[near_at][...],
            ins[code_at][...],
            ins[seen_at],
            chosen_ref,
            left_ref,
            emit,
        )
        fric_ref = ins[fric_at]
        asked = ins[asked_at][...].T
        own = [asked[i * node_pad : (i + 1) * node_pad] for i in range(4)]
        slip = friction_solve(
            fric_ref[:node_pad, :] + 0.5 * (kept[3] - kept[6]),
            fric_ref[node_pad:, :] + 0.5 * kept[0],
            *own,
        )
        wide_ref[...] = pad_rows(slip, LANES).T
        packed = wide_ref[pl.ds(0, slots // per_row, stride=per_row), :]
        for k in range(1, per_row):
            part = wide_ref[pl.ds(k, slots // per_row, stride=per_row), :]
            packed = packed + pltpu.roll(part, k * slot_lanes, 1)
        outs[back_at][...] = packed
        outs[slip_at][...] = slip
        outs.flush(slip_at)

    def final_kernel(ins, outs, moved_ref, trace_ref, turned_ref, mixed_ref, chosen_ref, left_ref):
        got_at = range(4)
        trace_table_at, turn_table_at, near_at, code_at, seen_at, asked_at, slip_at = range(4, 11)
        work_at, lift_at, kxi_at, flux_at, star_at, dofs_at = range(11, 17)

        def emit(q, value):
            turned_ref[q * node_pad : (q + 1) * node_pad, :] = value

        seen_across(
            [ins[i] for i in got_at],
            range(QUANT),
            ins[trace_table_at][...],
            ins[turn_table_at][...],
            ins[near_at][...],
            ins[code_at][...],
            ins[seen_at],
            chosen_ref,
            left_ref,
            emit,
        )
        asked = ins[asked_at][...].T
        wanted = one_hot(0, sides_all, asked_item(asked))
        slip_head, slip_rest = split(ins[slip_at][...])
        pushed = lax.dot_general(
            jnp.concatenate([slip_head, slip_rest], axis=0).astype(half),
            wanted,
            (((1,), (1,)), ((), ())),
            preferred_element_type=f32,
        )
        pushed = 2.0 * (pushed[:node_pad] + pushed[node_pad:])
        kxi_ref, lift_ref, work_ref = ins[kxi_at], ins[lift_at], ins[work_at]
        back_table = table(jnp.concatenate([kxi_ref[d] for d in range(DIMS)], axis=0))
        lift_table = jnp.concatenate(
            [table(pad_lanes(lift_ref[:, j, :].T, node_pad)) for j in range(FACES)], axis=1
        )
        trace_table = ins[trace_table_at][...]
        for q in range(QUANT):
            right = pieces(work_ref[q * basis : (q + 1) * basis, :])
            moved_ref[q] = product(back_table, right)
            trace_ref[q] = product(trace_table, right)
        flux_ref = ins[flux_at]
        for side in range(sides):
            lanes = slice(side * LANES, (side + 1) * LANES)
            for j in range(FACES):
                at = j * elems + side * LANES
                totals = flux_apply(
                    flux_ref,
                    0,
                    lambda q: trace_ref[q, j * node_pad : (j + 1) * node_pad, lanes],
                    j,
                    side,
                    [None] * QUANT,
                )
                totals = flux_apply(
                    flux_ref,
                    1,
                    lambda q: turned_ref[q * node_pad : (q + 1) * node_pad, at : at + LANES],
                    j,
                    side,
                    totals,
                )
                push = pushed[:, at : at + LANES]
                totals[3] = totals[3] - push
                totals[6] = totals[6] + push
                for p in range(QUANT):
                    mixed_ref[p, j * turn_depth : (j + 1) * turn_depth, lanes] = pieces(totals[p])
        star_ref, dofs_ref = ins[star_at], ins[dofs_at]
        out_ref = outs[0]
        for side in range(sides):
            lanes = slice(side * LANES, (side + 1) * LANES)

            def emit(p, value):
                rows = slice(p * basis, (p + 1) * basis)
                out_ref[rows, lanes] = dofs_ref[rows, lanes] + 0.25 * value

            star_apply(
                star_ref,
                lambda q, d: moved_ref[q, d * basis : (d + 1) * basis, lanes],
                side,
                emit,
            )
        for p in range(QUANT):
            rows = slice(p * basis, (p + 1) * basis)
            out_ref[rows, :] = out_ref[rows, :] + 0.25 * product(lift_table, mixed_ref[p])

    def return_kernel(ins, outs):
        place = ins[0][...]
        held = ins[1][...].T
        rows = slots // per_row
        lefts, picked = [], []
        for k in range(per_row):
            head, rest = split(held[k * slot_lanes : k * slot_lanes + node_pad])
            lefts.append(jnp.concatenate([head, rest], axis=0))
            picked.append(one_hot(0, rows, jnp.where(place % per_row == k, place // per_row, -1)))
        got = product(jnp.concatenate(lefts, axis=1).astype(half), jnp.concatenate(picked, axis=0))
        outs[0][...] = (got[:node_pad] + got[node_pad:])[:nodes]

    vmem = pltpu.VMEM
    proj_rows = jnp.transpose(face_proj, (2, 0, 1))
    lift_rows = jnp.transpose(face_lift, (1, 0, 2))
    asked, slot_of, work, *sends = call(
        predict_kernel,
        "predict",
        [
            kxi,
            dofs,
            star,
            fault_part.reshape(1, faults),
            fault_item.reshape(1, faults),
            shear_init,
            normal_init,
            state_var,
            slip_prev,
            send_list,
        ],
        [
            ((slots, LANES), f32, "hbm"),
            ((1, faults), jnp.int32, "vmem"),
            (dofs.shape, f32, "vmem"),
        ]
        + [((halo_rows, 2 * ghosts), f32, "any")] * 4,
        scratch=(
            vmem((DIMS * basis, depth), half),
            vmem((elems, 8 * ghosts), half),
            *[vmem((QUANT, DIMS * basis, LANES), f32)] * sides,
            *[vmem((QUANT, depth, LANES), half)] * sides,
        ),
        flops=5 * 2 * DIMS * basis * depth * QUANT * elems,
        moved=8_000_000,
    )

    asked = lax.all_to_all(
        asked.reshape(devices, slot_most, LANES), ("row", "col"), split_axis=0, concat_axis=0, tiled=True
    ).reshape(slots, LANES)

    def swapped(values, axis, first):
        pairs = [(i, i + 1) for i in range(first, lax.axis_size(axis) - 1, 2)]
        return lax.ppermute(values, axis, pairs + [(b, a) for a, b in pairs])

    arrived = [
        swapped(sends[0], "row", 0),
        swapped(sends[1], "row", 1),
        swapped(sends[2], "col", 0),
        swapped(sends[3], "col", 1),
    ]

    seen, fric, slot_seen, slot_near, slot_code, trace_table, turn_table, near, code = call(
        local_kernel,
        "local_terms",
        [proj_rows, neighbour, Kept(work), orient, orient_code, Kept(asked)],
        [
            ((QUANT * pair, sides_all), half, "vmem"),
            ((pair, slots), f32, "vmem"),
            ((len(first_q) * pair, slots), half, "vmem"),
            ((1, slots), jnp.int32, "vmem"),
            ((1, slots), jnp.int32, "vmem"),
            ((FACES * node_pad, depth), half, "vmem"),
            ((TURNS * node_pad, turn_depth), half, "vmem"),
            ((1, sides_all), jnp.int32, "vmem"),
            ((1, sides_all), jnp.int32, "vmem"),
        ],
        scratch=(
            vmem((QUANT * pair, sides_all), half),
            vmem((sides_all, sides_all), half),
            vmem((sides_all, slots), half),
        ),
        flops=2 * QUANT * pair * sides_all * sides_all,
        moved=8_000_000,
    )

    back, slip = call(
        friction_kernel,
        "friction",
        [
            Kept(one)
            for one in (*arrived, trace_table, turn_table, slot_near, slot_code, slot_seen, fric, asked)
        ],
        [((slots // per_row, LANES), f32, "any"), ((node_pad, slots), f32, "vmem")],
        scratch=(
            vmem((FACES * ghost_all, slots), half),
            vmem((len(first_q) * pair, FACES * ghost_all), half),
            vmem((slots, LANES), f32),
        ),
        flops=2 * len(first_q) * pair * sides_all * slots,
        moved=4_000_000,
    )
    back = lax.all_to_all(
        back.reshape(devices, *chunk_shape), ("row", "col"), split_axis=0, concat_axis=0, tiled=True
    ).reshape(slots // per_row, LANES)

    (dofs_next,) = call(
        final_kernel,
        "final_terms",
        [
            *(Kept(one) for one in arrived),
            Kept(trace_table),
            Kept(turn_table),
            Kept(near),
            Kept(code),
            Kept(seen),
            Kept(asked),
            Kept(slip),
            Kept(work),
            lift_rows,
            kxi,
            flux_mats,
            star,
            dofs,
        ],
        [(dofs.shape, f32, "any")],
        scratch=(
            vmem((QUANT, DIMS * basis, elems), f32),
            vmem((QUANT, FACES * node_pad, elems), f32),
            vmem((QUANT * node_pad, sides_all), f32),
            vmem((QUANT, FACES * turn_depth, elems), half),
            vmem((FACES * ghost_all, sides_all), half),
            vmem((QUANT * pair, FACES * ghost_all), half),
        ),
        flops=2 * QUANT * pair * sides_all * sides_all,
        moved=8_000_000,
    )

    (slip_rate,) = call(
        return_kernel,
        "fault_return",
        [Kept(slot_of), Kept(back)],
        [((nodes, faults), f32, "any")],
        flops=2 * pair * slots * faults,
        moved=200_000,
    )
    return dofs_next, slip_rate


def solution(mesh):
    across = ("row", "col")
    placed = (
        P(None, across),
        P(None, across),
        P(None, across),
        P(),
        P(),
        P(),
        P(),
        P(None, across),
        P(None, across),
        P(None, across),
        P(across, None),
        P(across),
        P(None, across),
        P(None, across),
        P(None, across),
        P(None, across),
    )
    return jax.shard_map(
        per_device,
        mesh=mesh,
        in_specs=placed,
        out_specs=(P(None, across), P(None, across)),
        check_vma=False,
    )
```
